128 devices in a mesh: leaf: 8 (over x, core), blk: 16 (over z, y).
Axes of the slice: x: 4, y: 4, z: 4, core: 2. Of those that a mesh axis runs over, the one named last changes fastest.
Arguments:
- right_side: float32 [8, 16, 240, 128], P('leaf', 'blk'), may hold values from -6 to 6
- inverse_blocks: bfloat16 [8, 16, 240, 2048], P('leaf', 'blk'), may hold values from -0.125 to 0.125
- coupling: bfloat16 [8, 16, 544, 1024], P('leaf', 'blk'), may hold values from -0.0625 to 0.0625
- update_rows: int32 [34, 1024], replicated, may hold values from 0 to 2047, as said below
Outputs:
- solution: float32 [8, 16, 240, 128], P('leaf', 'blk')
The draws below stay inside these ranges and needn't reach their ends.
Inputs may be any that keep to these rules, and one draw needn't show every extreme that they name: `update_rows`: the 1024 entries of each row are distinct.
All inputs are finite; a program needn't handle non-finite values.
Results may differ from the reference program's by a relative error of at most 0.0075.
Values may be sent and summed in bfloat16 or wider, within the bound.
A program may use at most 64 MiB of HBM per device.

```python
import jax
import jax.numpy as jnp
from jax import lax

W = 2048
UPD = 1024
CASES = 128
HEIGHT = 3
ROWS_DEV = 240
OFF_ROWS = 544
PAIRS = 34
N_LEAF = 8
N_BLK = 16


def draw_update_rows(key, part):
    keys = jax.random.split(key, PAIRS)
    return jax.vmap(lambda single: jax.random.permutation(single, W)[:UPD])(keys).astype(jnp.int32)


def steps_of(key, shape, cuts, low, largest):
    loudness = 1.0
    for dim, shards_of in cuts:
        draws = jax.random.uniform(jax.random.fold_in(jax.random.fold_in(key, 6), dim), (shards_of,), jnp.float32, low / len(cuts), largest / len(cuts))
        loudness = loudness * jnp.repeat(jnp.exp(draws), shape[dim] // shards_of).reshape((-1,) + (1,) * (len(shape) - 1 - dim))
    return loudness


def noise(stream_key, extent, deviation, bound, cuts=(), kind=jnp.bfloat16):
    values = deviation * jax.random.normal(stream_key, extent, jnp.float32)
    if cuts:
        values = values * steps_of(stream_key, extent, cuts, -0.22, 0.18)
    return jnp.clip(values, -bound, bound).astype(kind)


def setup_inputs(seed: int = 0) -> dict:
    arg_keys = jax.random.split(jax.random.key(seed), 5)
    return {
        "right_side": noise(arg_keys[0], (N_LEAF, N_BLK, ROWS_DEV, CASES), 1.0, 6.0, ((0, 8), (1, 16)), jnp.float32),
        "inverse_blocks": noise(arg_keys[1], (N_LEAF, N_BLK, ROWS_DEV, W), W ** -0.5, 0.125, ((0, 8), (1, 16))),
        "coupling": noise(arg_keys[2], (N_LEAF, N_BLK, OFF_ROWS, UPD), (4 * W) ** -0.5, 0.0625, ((0, 8), (1, 16))),
        "update_rows": draw_update_rows(jax.random.fold_in(arg_keys[4], 71), 0),
    }


def level_span(level_no):
    row_start = 0
    for lower_level in range(level_no):
        row_start += W // (N_BLK * 2 ** lower_level)
    return row_start, W // (N_BLK * 2 ** level_no)


def level_rows(stacked, level_no):
    row_start, row_count = level_span(level_no)
    section = stacked[:, :, row_start:row_start + row_count, :]
    return section.reshape(N_LEAF >> level_no, W, stacked.shape[-1])


def coupling_rows(coupling, level_no, ancestor):
    row_start = 0
    for lower_level in range(HEIGHT):
        row_count = W // (N_BLK * 2 ** lower_level)
        for upper_level in range(lower_level + 1, HEIGHT + 1):
            if lower_level == level_no and upper_level == ancestor:
                section = coupling[:, :, row_start:row_start + row_count, :]
                return section.reshape(N_LEAF >> level_no, W, coupling.shape[-1])
            row_start += row_count
    return None


def update_lists(update_rows, level_no, ancestor):
    pair_base = 0
    for lower_level in range(level_no):
        pair_base += (N_LEAF >> lower_level) * (HEIGHT - lower_level)
    node_count = N_LEAF >> level_no
    node_ids = jnp.arange(node_count, dtype=jnp.int32)
    pair_rows = pair_base + node_ids * (HEIGHT - level_no) + (ancestor - level_no - 1)
    parents = node_ids // (2 ** (ancestor - level_no))
    return update_rows[pair_rows], parents


def rounded(values):
    return lax.optimization_barrier(values.astype(jnp.bfloat16)).astype(jnp.float32)


def reference(right_side, inverse_blocks, coupling, update_rows):
    pending = {}
    y_levels = []
    for level_no in range(HEIGHT + 1):
        residual = level_rows(right_side, level_no)
        if level_no in pending:
            residual = residual - pending[level_no]
        inverse = level_rows(inverse_blocks, level_no).astype(jnp.float32)
        y_rows = jnp.einsum("nwv,nvk->nwk", inverse, rounded(residual))
        y_levels.append(y_rows)
        y_round = rounded(y_rows)
        for ancestor in range(level_no + 1, HEIGHT + 1):
            blocks = coupling_rows(coupling, level_no, ancestor).astype(jnp.float32)
            contrib = jnp.einsum("nwu,nwk->nuk", blocks, y_round)
            row_lists, parents = update_lists(update_rows, level_no, ancestor)
            summed = pending.get(ancestor, jnp.zeros((N_LEAF >> ancestor, W, CASES), jnp.float32))
            pending[ancestor] = summed.at[parents[:, None], row_lists].add(contrib)
    solved = {}
    sections = [None] * (HEIGHT + 1)
    for level_no in range(HEIGHT, -1, -1):
        z_rows = y_levels[level_no]
        for ancestor in range(level_no + 1, HEIGHT + 1):
            blocks = coupling_rows(coupling, level_no, ancestor).astype(jnp.float32)
            row_lists, parents = update_lists(update_rows, level_no, ancestor)
            picked = solved[ancestor][parents[:, None], row_lists].astype(jnp.float32)
            z_rows = z_rows - jnp.einsum("nwu,nuk->nwk", blocks, picked)
        inverse = level_rows(inverse_blocks, level_no).astype(jnp.float32)
        x_rows = jnp.einsum("nvw,nvk->nwk", inverse, rounded(z_rows))
        row_start, row_count = level_span(level_no)
        sections[level_no] = x_rows.reshape(N_LEAF, N_BLK, row_count, CASES)
        solved[level_no] = x_rows.astype(jnp.bfloat16)
    return jnp.concatenate(sections, axis=2)
```

```python
import functools

import jax
import jax.numpy as jnp
from jax import lax
from jax.experimental import pallas as pl
from jax.experimental.pallas import tpu as pltpu
from jax.sharding import PartitionSpec as P

MESH = pl.DeviceIdType.MESH
F32, BF16 = jnp.float32, jnp.bfloat16

W = 2048
UPD = 1024
CASES = 128
HALF = 64
BLKS = 16
BLK = W // BLKS
ROWS = (128, 64, 32, 16)
STARTS = (0, 128, 192, 224)
COUP = {(0, 1): 0, (0, 2): 128, (0, 3): 256, (1, 2): 384, (1, 3): 448, (2, 3): 512}
PAIR_BASE = (0, 24, 32)

NAMES = (
    ["ag0", "d1", "d2", "d3", "c12", "c13", "c23", "b1", "b2", "b3", "x01", "x02", "x03", "y0"]
    + [f"rsf{l}" for l in (1, 2, 3)]
    + ["xf2", "xf3"]
    + [f"agf{l}" for l in (1, 2, 3)]
    + [f"rsb{l}" for l in (1, 2, 3)]
    + [f"agb{l}" for l in (1, 2, 3)]
    + ["sx", "rs0", "xo1", "xo2", "xo3"]
)
SEM = {name: i for i, name in enumerate(NAMES)}
LOCALS = ["rhs", "d0", "idx", "c01", "c02", "c03", "d1", "d2", "d3", "c12", "c13", "c23", "b1", "b2", "b3"]
LSEM = {name: i for i, name in enumerate(LOCALS)}


def dot_nt(a, b):
    return lax.dot_general(a, b, (((1,), (1,)), ((), ())), preferred_element_type=F32)


def dot_nn(a, b):
    return jnp.dot(a, b, preferred_element_type=F32)


def far_first(i):
    return jnp.where(i < 2, 2 - i, jnp.where(i == 2, 3, 0))


def kernel(
    rhs_hbm, d_hbm, c_hbm, u_hbm, out,
    rhs0, idx, d0, d1, d2, d3, p1, p2, p3, c01, c02, c03, c12, c13, c23,
    x0, x12, x13, x23, b1, b2, b3, bt, ball0, y0r, y0b, ysib,
    sf1, sf2, sf3, rf1, rf2, rf3, vf1, vf2, vf3,
    sb1, sb2, sb3, rb1, rb2, rb3, vb1, vb2, vb3,
    xs, xr2, xr3, pend2, pend3, ssend, srecv, z0r, s0, r0, xo1, xo2, xo3, tmp,
    ssem, rsem, lsem,
):
    lf, bk = lax.axis_index("leaf"), lax.axis_index("blk")
    core = lax.rem(lf, 2)
    mine = pl.multiple_of(core * HALF, HALF)
    other = pl.multiple_of((1 - core) * HALF, HALF)
    zc, yc = lax.div(bk, 4), lax.rem(bk, 4)
    sib = (lf ^ 1, bk)
    draw, dperm = (d0, d1, d2, d3), (None, p1, p2, p3)
    ball = (None, b1, b2, b3)
    sends = []

    def rcopy(src, dst, name, dev):
        i = SEM[name]
        return pltpu.make_async_remote_copy(
            src_ref=src, dst_ref=dst, send_sem=ssem.at[i], recv_sem=rsem.at[i], device_id=dev, device_id_type=MESH
        )

    def arrived(ref, name):
        rcopy(ref, ref, name, sib).wait_recv()

    def lcopy(src, dst, name):
        return pltpu.make_async_copy(src, dst, lsem.at[LSEM[name]])

    def plane_peer(k):
        z = lax.rem(zc + far_first(lax.div(k, 4)), 4)
        y = lax.rem(yc + far_first(lax.rem(k, 4)), 4)
        return z * 4 + y

    def plane_push(name, src_of, dst_of):
        def body(k, carry):
            p = plane_peer(k)
            rcopy(src_of(k, p), dst_of(k, p), name, (lf, p)).start()
            return carry

        lax.fori_loop(0, BLKS - 1, body, 0)

    local = {}

    def fetch(name, src, dst):
        local[name] = lcopy(src, dst, name)
        local[name].start()

    fetch("rhs", rhs_hbm.at[pl.ds(0, ROWS[0])], rhs0)
    fetch("idx", u_hbm, idx)
    fetch("c01", c_hbm.at[pl.ds(COUP[0, 1], 128)], c01)
    fetch("d0", d_hbm.at[pl.ds(0, 128)], d0)

    barrier = pltpu.get_barrier_semaphore()

    def greet(k, carry):
        pl.semaphore_signal(barrier, inc=1, device_id=(lf, plane_peer(k)), device_id_type=MESH)
        return carry

    lax.fori_loop(0, BLKS - 1, greet, 0)

    def greet_leaf(q, carry):
        pl.semaphore_signal(barrier, inc=1, device_id=(lf ^ q, bk), device_id_type=MESH)
        return carry

    lax.fori_loop(1, 8, greet_leaf, 0)
    local["rhs"].wait()
    ball0[bk] = rhs0[...].T.astype(BF16)
    pl.semaphore_wait(barrier, BLKS - 1 + 7)

    plane_push("ag0", lambda k, p: ball0.at[bk], lambda k, p: ball0.at[bk])
    sends.append(("ag0", ball0.at[pl.ds(0, BLKS - 1)]))

    def spread(name, level, hbm, start, ref):
        count = ROWS[level]
        member = lf & ((1 << level) - 1)
        place = ref.at[pl.ds(pl.multiple_of(member * count, count), count)]
        src = hbm.at[pl.ds(start, count)]

        def body(q, carry):
            rcopy(src, place, name, (lf ^ q, bk)).start()
            return carry

        lax.fori_loop(1, 1 << level, body, 0)
        fetch(name, src, place)
        sends.append((name, ref.at[pl.ds(0, BLK - count)]))

    def spread_done(name, level, ref):
        local[name].wait()
        arrived(ref.at[pl.ds(0, BLK - ROWS[level])], name)

    spread("b1", 1, rhs_hbm, STARTS[1], b1)
    spread("d1", 1, d_hbm, STARTS[1], d1)
    spread("c12", 1, c_hbm, COUP[1, 2], c12)
    fetch("c02", c_hbm.at[pl.ds(COUP[0, 2], 128)], c02)
    fetch("c03", c_hbm.at[pl.ds(COUP[0, 3], 128)], c03)

    def expand(c_ref, level, ancestor, store):
        node = lax.div(lf, 1 << level)
        row = PAIR_BASE[level] + node * (3 - level) + (ancestor - level - 1)
        listed = idx[pl.ds(row, 1), :]
        count = ROWS[ancestor]
        bits = count.bit_length() - 1
        place = ((listed >> bits) & (BLKS - 1)) * BLK + (listed >> (bits + 4)) * count + (listed & (count - 1))
        rows = c_ref[...]

        def body(q, carry):
            target = lax.broadcasted_iota(jnp.int32, (256, UPD), 0) + q * 256
            hot = jnp.where(target == place, 1.0, 0.0).astype(BF16)
            store(pl.ds(pl.multiple_of(q * 256, 256), 256), dot_nt(rows, hot).astype(BF16))
            return carry

        lax.fori_loop(0, W // 256, body, 0)

    def expand0(ancestor, c_ref):
        a = ancestor - 1

        def store(cols, value):
            x0[a, pl.ds(0, 128), cols] = value

        expand(c_ref, 0, ancestor, store)
        rcopy(x0.at[a, pl.ds(0, 128)], x0.at[a, pl.ds(128, 128)], f"x0{ancestor}", sib).start()
        sends.append((f"x0{ancestor}", x0.at[a, pl.ds(0, 128)]))

    def expand0_done(ancestor):
        arrived(x0.at[ancestor - 1, pl.ds(128, 128)], f"x0{ancestor}")

    def expand_up(level, ancestor, c_ref, x_ref):
        def store(cols, value):
            x_ref[:, cols] = value

        expand(c_ref, level, ancestor, store)

    def permute(level):
        count = ROWS[level]
        lane = lax.broadcasted_iota(jnp.int32, (BLK, BLK), 1)
        for b in range(BLKS):
            total = None
            for m in range(1 << level):
                col = (m * BLKS + b) * count
                tile = draw[level][:, col // BLK * BLK : (col // BLK + 1) * BLK].astype(F32)
                turn = (m * count - col % BLK) % BLK
                if turn:
                    tile = pltpu.roll(tile, turn, 1)
                total = tile if total is None else jnp.where(lane >= m * count, tile, total)
            dperm[level][:, b * BLK : (b + 1) * BLK] = total.astype(BF16)

    def own_rhs(level):
        bt[level - 1] = ball[level][...].T

    def whole(ref):
        return jnp.concatenate([ref[b] for b in range(BLKS)], axis=1)

    def scatter(name, value, s_ref, r_ref):
        for b in range(BLKS):
            s_ref[b] = value[:, b * BLK : (b + 1) * BLK].astype(BF16)
        plane_push(name, lambda k, p: s_ref.at[p], lambda k, p: r_ref.at[k])
        sends.append((name, r_ref))

    def scatter_done(name, s_ref, r_ref):
        arrived(r_ref, name)
        total = s_ref[bk].astype(F32)
        for k in range(BLKS - 1):
            total = total + r_ref[k].astype(F32)
        return total

    def gather(name, value, v_ref):
        v_ref[bk] = value.astype(BF16)
        plane_push(name, lambda k, p: v_ref.at[bk], lambda k, p: v_ref.at[bk])
        sends.append((name, v_ref.at[pl.ds(0, BLKS - 1)]))

    def gather_done(name, v_ref):
        arrived(v_ref.at[pl.ds(0, BLKS - 1)], name)
        return whole(v_ref)

    local["idx"].wait()
    local["c01"].wait()
    expand0(1, c01)

    spread("b2", 2, rhs_hbm, STARTS[2], b2)
    spread("d2", 2, d_hbm, STARTS[2], d2)
    spread("c13", 1, c_hbm, COUP[1, 3], c13)
    spread("c23", 2, c_hbm, COUP[2, 3], c23)
    spread("b3", 3, rhs_hbm, STARTS[3], b3)
    spread("d3", 3, d_hbm, STARTS[3], d3)

    local["d0"].wait()
    v = gather_done("ag0", ball0)
    y0 = dot_nt(v, d0[...])
    y0r[...] = y0
    y0b[...] = y0.astype(BF16)
    rcopy(y0b.at[pl.ds(other, HALF)], ysib, "y0", sib).start()
    sends.append(("y0", ysib))
    expand0_done(1)
    arrived(ysib, "y0")
    y0c = jnp.concatenate([y0b[pl.ds(mine, HALF), :], ysib[...]], axis=1)
    scatter("rsf1", dot_nn(y0c, x0[0]), sf1, rf1)

    spread_done("b1", 1, b1)
    own_rhs(1)
    spread_done("d1", 1, d1)
    permute(1)
    local["c02"].wait()
    expand0(2, c02)
    total = scatter_done("rsf1", sf1, rf1)
    gather("agf1", bt[0, pl.ds(mine, HALF), :] - total, vf1)
    spread_done("c12", 1, c12)
    expand_up(1, 2, c12, x12)
    expand0_done(2)
    pend2[...] = dot_nn(y0c, x0[1])
    v = gather_done("agf1", vf1)
    y1 = dot_nt(v, p1[...])
    y1b = y1.astype(BF16)
    scatter("rsf2", pend2[...] + dot_nn(y1b, x12[...]), sf2, rf2)

    spread_done("b2", 2, b2)
    own_rhs(2)
    spread_done("d2", 2, d2)
    permute(2)
    local["c03"].wait()
    expand0(3, c03)
    total = scatter_done("rsf2", sf2, rf2).astype(BF16)
    xs[0] = total
    rcopy(xs.at[0], xr2, "xf2", (lf ^ 2, bk)).start()
    sends.append(("xf2", xr2))
    expand0_done(3)
    arrived(xr2, "xf2")
    total = total.astype(F32) + xr2[...].astype(F32)
    gather("agf2", bt[1, pl.ds(mine, HALF), :] - total, vf2)
    spread_done("c23", 2, c23)
    expand_up(2, 3, c23, x23)
    spread_done("c13", 1, c13)
    expand_up(1, 3, c13, x13)
    pend3[...] = dot_nn(y0c, x0[2]) + dot_nn(y1b, x13[...])
    v = gather_done("agf2", vf2)
    y2 = dot_nt(v, p2[...])
    lane = lax.broadcasted_iota(jnp.int32, (HALF, BLK), 1)
    half = lax.rem(lax.div(lf, 2), 2)
    y2b = jnp.where(lax.div(lane, HALF) == half, y2, 0.0).astype(BF16)
    scatter("rsf3", pend3[...] + dot_nn(y2b, x23[...]), sf3, rf3)

    spread_done("b3", 3, b3)
    own_rhs(3)
    spread_done("d3", 3, d3)
    permute(3)
    total = scatter_done("rsf3", sf3, rf3).astype(BF16)
    xs[1] = total

    def to_planes(q, carry):
        rcopy(xs.at[1], xr3.at[q - 1], "xf3", (lf ^ (2 * q), bk)).start()
        return carry

    lax.fori_loop(1, 4, to_planes, 0)
    sends.append(("xf3", xr3))
    arrived(xr3, "xf3")
    total = total.astype(F32)
    for q in range(3):
        total = total + xr3[q].astype(F32)
    gather("agf3", bt[2, pl.ds(mine, HALF), :] - total, vf3)
    v = gather_done("agf3", vf3)
    y3 = dot_nt(v, p3[...])

    def keep(level, value, xo_ref):
        xo_ref[pl.ds(mine, HALF), :] = value
        rcopy(xo_ref.at[pl.ds(mine, HALF)], xo_ref.at[pl.ds(mine, HALF)], f"xo{level}", sib).start()
        sends.append((f"xo{level}", xo_ref.at[pl.ds(0, HALF)]))

    def write(level, xo_ref):
        arrived(xo_ref.at[pl.ds(0, HALF)], f"xo{level}")
        count = ROWS[level]
        member = lf & ((1 << level) - 1)
        tmp[...] = xo_ref[...].T
        out[pl.ds(STARTS[level], count), :] = tmp[pl.ds(pl.multiple_of(member * count, count), count), :]

    scatter("rsb3", dot_nn(y3.astype(BF16), p3[...]), sb3, rb3)
    total = scatter_done("rsb3", sb3, rb3)
    gather("agb3", total, vb3)
    keep(3, total, xo3)
    v3 = gather_done("agb3", vb3)

    z = y2 - dot_nt(v3, x23[...])
    scatter("rsb2", dot_nn(z.astype(BF16), p2[...]), sb2, rb2)
    z1 = y1 - dot_nt(v3, x13[...])
    t0 = dot_nt(v3, x0[2])
    write(3, xo3)
    total = scatter_done("rsb2", sb2, rb2)
    gather("agb2", total, vb2)
    keep(2, total, xo2)
    v = gather_done("agb2", vb2)

    z1 = z1 - dot_nt(v, x12[...])
    scatter("rsb1", dot_nn(z1.astype(BF16), p1[...]), sb1, rb1)
    t0 = t0 + dot_nt(v, x0[1])
    write(2, xo2)
    total = scatter_done("rsb1", sb1, rb1)
    gather("agb1", total, vb1)
    keep(1, total, xo1)
    v = gather_done("agb1", vb1)

    t0 = t0 + dot_nt(v, x0[0])
    ssend[...] = t0[:, BLK:].astype(BF16)
    rcopy(ssend, srecv, "sx", sib).start()
    sends.append(("sx", ssend))
    z0r[pl.ds(mine, HALF), :] = y0r[pl.ds(mine, HALF), :] - t0[:, :BLK]
    arrived(srecv, "sx")
    z0r[pl.ds(other, HALF), :] = y0r[pl.ds(other, HALF), :] - srecv[...].astype(F32)
    scatter("rs0", dot_nn(z0r[...].astype(BF16), d0[...]), s0, r0)
    write(1, xo1)
    total = scatter_done("rs0", s0, r0)
    out[pl.ds(0, 128), :] = total.T
    for name, ref in sends:
        rcopy(ref, ref, name, sib).wait_send()


def local(right_side, inverse_blocks, coupling, update_rows):
    def vm(*shape, t=BF16):
        return pltpu.VMEM(shape, t)

    block = (HALF, BLK)
    scratch = (
        [vm(128, CASES, t=F32), vm(34, UPD, t=jnp.int32)]
        + [vm(128, W)] * 7
        + [vm(128, UPD)] * 6
        + [vm(3, 256, W)]
        + [vm(128, W)] * 3
        + [vm(128, CASES, t=F32)] * 3
        + [vm(3, CASES, BLK, t=F32), vm(BLKS, CASES, BLK)]
        + [vm(CASES, BLK, t=F32), vm(CASES, BLK), vm(*block)]
        + ([vm(BLKS, *block)] * 3 + [vm(BLKS - 1, *block)] * 3 + [vm(BLKS, *block)] * 3) * 2
        + [vm(2, *block), vm(*block), vm(3, *block)]
        + [vm(HALF, W, t=F32)] * 2
        + [vm(*block), vm(*block), vm(CASES, BLK, t=F32)]
        + [vm(BLKS, CASES, BLK), vm(BLKS - 1, CASES, BLK)]
        + [vm(CASES, BLK, t=F32)] * 3
        + [vm(BLK, CASES, t=F32)]
        + [pltpu.SemaphoreType.DMA((len(NAMES),))] * 2
        + [pltpu.SemaphoreType.DMA((len(LOCALS),))]
    )
    result = pl.pallas_call(
        kernel,
        out_shape=jax.ShapeDtypeStruct((240, CASES), F32),
        in_specs=[pl.BlockSpec(memory_space=pl.ANY)] * 4,
        out_specs=pl.BlockSpec(memory_space=pltpu.VMEM),
        scratch_shapes=scratch,
        compiler_params=pltpu.CompilerParams(
            collective_id=0, has_side_effects=True, vmem_limit_bytes=48 * 1024 * 1024
        ),
        name="tree_solve",
    )(right_side[0, 0], inverse_blocks[0, 0], coupling[0, 0], update_rows)
    return result[None, None]


def solution(mesh):
    in_specs = (
        P("leaf", "blk", None, None),
        P("leaf", "blk", None, None),
        P("leaf", "blk", None, None),
        P(),
    )
    out_specs = P("leaf", "blk", None, None)
    return jax.shard_map(local, mesh=mesh, in_specs=in_specs, out_specs=out_specs, check_vma=False)
```

```python
import functools

import jax
import jax.numpy as jnp
from jax import lax
from jax.experimental import pallas as pl
from jax.experimental.pallas import tpu as pltpu
from jax.sharding import PartitionSpec as P

MESH = pl.DeviceIdType.MESH
F32, BF16 = jnp.float32, jnp.bfloat16

W = 2048
UPD = 1024
CASES = 128
HALF = 64
PART = 32
BLKS = 16
BLK = W // BLKS
ROWS = (128, 64, 32, 16)
STARTS = (0, 128, 192, 224)
COUP = {(0, 1): 0, (0, 2): 128, (0, 3): 256, (1, 2): 384, (1, 3): 448, (2, 3): 512}
PAIR_BASE = (0, 24, 32)

NAMES = (
    ["ag0a", "ag0b", "x01", "x02", "x03", "y0"]
    + [f"{name}{way}" for name in ("d1", "c12", "c13", "b1", "d2", "c23", "b2", "d3", "b3") for way in ("", "s")]
    + [f"{name}{l}{h}" for name in ("rsf", "agf", "rsb", "agb") for l in (1, 2, 3) for h in (0, 1)]
    + [f"{name}{h}" for name in ("xf2", "xf3", "sx", "rs0a", "rs0b") for h in (0, 1)]
    + ["rsp3", "xp3", "xo1", "xo2", "xo3"]
)
SEM = {name: i for i, name in enumerate(NAMES)}
LOCALS = ["rhs", "d0", "idx", "c01", "c02", "c03", "d1", "d2", "d3", "c12", "c13", "c23", "b1", "b2", "b3"]
LSEM = {name: i for i, name in enumerate(LOCALS)}


def dot_nt(a, b):
    return lax.dot_general(a, b, (((1,), (1,)), ((), ())), preferred_element_type=F32)


def dot_nn(a, b):
    return jnp.dot(a, b, preferred_element_type=F32)


def far_first(i):
    return jnp.where(i < 2, 2 - i, jnp.where(i == 2, 3, 0))


def kernel(
    rhs_hbm, d_hbm, c_hbm, u_hbm, out,
    rhs0, idx, d0, d1, d2, d3, p1, p2, p3, c01, c02, c03, c12, c13, c23,
    x0, x12, x13, x23, b1, b2, b3, bt, ball0, y0r, y0b, ysib,
    sf1, sf2, sf3, rf1, rf2, rf3, vf1, vf2, vf3,
    sb1, sb2, sb3, rb1, rb2, rb3, vb1, vb2, vb3,
    xs, xr2, xr3, xp, xp3, sp3, rp3, ssend, srecv, s0, r0, xo1, xo2, xo3, tmp,
    ssem, rsem, lsem,
):
    lf, bk = lax.axis_index("leaf"), lax.axis_index("blk")
    core = lax.rem(lf, 2)
    mine = pl.multiple_of(core * HALF, HALF)
    other = pl.multiple_of((1 - core) * HALF, HALF)
    zc, yc = lax.div(bk, 4), lax.rem(bk, 4)
    sib = (lf ^ 1, bk)
    draw, dperm = (d0, d1, d2, d3), (None, p1, p2, p3)
    ball = (None, b1, b2, b3)
    sends = []

    def rcopy(src, dst, name, dev):
        i = SEM[name]
        return pltpu.make_async_remote_copy(
            src_ref=src, dst_ref=dst, send_sem=ssem.at[i], recv_sem=rsem.at[i], device_id=dev, device_id_type=MESH
        )

    def arrived(ref, name):
        rcopy(ref, ref, name, sib).wait_recv()

    def lcopy(src, dst, name):
        return pltpu.make_async_copy(src, dst, lsem.at[LSEM[name]])

    def plane_peer(k):
        z = lax.rem(zc + far_first(lax.div(k, 4)), 4)
        y = lax.rem(yc + far_first(lax.rem(k, 4)), 4)
        return z * 4 + y

    def plane_push(name, src_of, dst_of):
        def body(k, carry):
            p = plane_peer(k)
            rcopy(src_of(k, p), dst_of(k, p), name, (lf, p)).start()
            return carry

        lax.fori_loop(0, BLKS - 1, body, 0)

    local = {}

    def fetch(name, src, dst):
        local[name] = lcopy(src, dst, name)
        local[name].start()

    fetch("rhs", rhs_hbm.at[pl.ds(0, ROWS[0])], rhs0)
    fetch("idx", u_hbm, idx)
    fetch("c01", c_hbm.at[pl.ds(COUP[0, 1], 128)], c01)
    fetch("d0", d_hbm.at[pl.ds(0, 128)], d0)

    barrier = pltpu.get_barrier_semaphore()

    def greet(k, carry):
        pl.semaphore_signal(barrier, inc=1, device_id=(lf, plane_peer(k)), device_id_type=MESH)
        return carry

    lax.fori_loop(0, BLKS - 1, greet, 0)

    def greet_leaf(q, carry):
        pl.semaphore_signal(barrier, inc=1, device_id=(lf ^ q, bk), device_id_type=MESH)
        return carry

    lax.fori_loop(1, 8, greet_leaf, 0)
    local["rhs"].wait()
    ball0[bk] = rhs0[...].T.astype(BF16)
    pl.semaphore_wait(barrier, BLKS - 1 + 7)

    for name, half in (("ag0a", other), ("ag0b", mine)):
        part = ball0.at[bk, pl.ds(half, HALF)]
        plane_push(name, lambda k, p: part, lambda k, p: part)
        sends.append((name, ball0.at[pl.ds(0, BLKS - 1), pl.ds(0, HALF)]))

    def place_of(level, ref, q):
        count = ROWS[level]
        member = (lf ^ q) & ((1 << level) - 1)
        return ref.at[pl.ds(pl.multiple_of(member * count, count), count)]

    def spread(name, level, hbm, start, ref):
        count = ROWS[level]
        src = hbm.at[pl.ds(start, count)]
        for q in range(2, 1 << level, 2):
            rcopy(src, place_of(level, ref, 0), name, (lf ^ q, bk)).start()
        if level == 1:
            rcopy(src, place_of(level, ref, 0), name + "s", sib).start()
            sends.append((name + "s", ref.at[pl.ds(0, count)]))
        else:
            sends.append((name, ref.at[pl.ds(0, BLK // 2 - count)]))
        fetch(name, src, place_of(level, ref, 0))

    def forward(name, level, ref):
        count = ROWS[level]
        local[name].wait()
        arrived(ref.at[pl.ds(0, BLK // 2 - count)], name)
        for q in range(0, 1 << level, 2):
            rcopy(place_of(level, ref, q), place_of(level, ref, q), name + "s", sib).start()
        sends.append((name + "s", ref.at[pl.ds(0, BLK // 2)]))

    def spread_done(name, level, ref):
        if level == 1:
            local[name].wait()
        arrived(ref.at[pl.ds(0, BLK // 2)], name + "s")

    spread("b1", 1, rhs_hbm, STARTS[1], b1)
    spread("d1", 1, d_hbm, STARTS[1], d1)
    fetch("c02", c_hbm.at[pl.ds(COUP[0, 2], 128)], c02)
    fetch("c03", c_hbm.at[pl.ds(COUP[0, 3], 128)], c03)
    spread("c12", 1, c_hbm, COUP[1, 2], c12)
    spread("b2", 2, rhs_hbm, STARTS[2], b2)
    spread("d2", 2, d_hbm, STARTS[2], d2)
    spread("c23", 2, c_hbm, COUP[2, 3], c23)
    spread("c13", 1, c_hbm, COUP[1, 3], c13)

    def expand(c_ref, level, ancestor, store):
        node = lax.div(lf, 1 << level)
        row = PAIR_BASE[level] + node * (3 - level) + (ancestor - level - 1)
        listed = idx[pl.ds(row, 1), :]
        count = ROWS[ancestor]
        bits = count.bit_length() - 1
        place = ((listed >> bits) & (BLKS - 1)) * BLK + (listed >> (bits + 4)) * count + (listed & (count - 1))
        rows = c_ref[...]

        for q in range(W // 256):
            target = lax.broadcasted_iota(jnp.int32, (256, UPD), 0) + q * 256
            hot = jnp.where(target == place, 1.0, 0.0).astype(BF16)
            store(slice(q * 256, (q + 1) * 256), dot_nt(rows, hot).astype(BF16))

    def expand0(ancestor, c_ref):
        a = ancestor - 1

        def store(cols, value):
            x0[a, 0:128, cols] = value

        expand(c_ref, 0, ancestor, store)
        rcopy(x0.at[a, pl.ds(0, 128)], x0.at[a, pl.ds(128, 128)], f"x0{ancestor}", sib).start()
        sends.append((f"x0{ancestor}", x0.at[a, pl.ds(0, 128)]))

    def expand0_done(ancestor):
        arrived(x0.at[ancestor - 1, pl.ds(128, 128)], f"x0{ancestor}")

    def expand_up(level, ancestor, c_ref, x_ref):
        def store(cols, value):
            x_ref[:, cols] = value

        expand(c_ref, level, ancestor, store)

    def permute(level):
        count = ROWS[level]
        lane = lax.broadcasted_iota(jnp.int32, (BLK, BLK), 1)
        for b in range(BLKS):
            total = None
            for m in range(1 << level):
                col = (m * BLKS + b) * count
                tile = draw[level][:, col // BLK * BLK : (col // BLK + 1) * BLK].astype(F32)
                turn = (m * count - col % BLK) % BLK
                if turn:
                    tile = pltpu.roll(tile, turn, 1)
                total = tile if total is None else jnp.where(lane >= m * count, tile, total)
            dperm[level][:, b * BLK : (b + 1) * BLK] = total.astype(BF16)

    def own_rhs(level):
        bt[level - 1] = ball[level][...].T

    def whole(ref, h):
        return jnp.concatenate([ref[h, b] for b in range(BLKS)], axis=1)

    def part(h):
        return pl.ds(pl.multiple_of(mine + h * PART, PART), PART)

    def rows_of(value, h):
        return value[h * PART : (h + 1) * PART]

    def both(values):
        return jnp.concatenate(values, axis=0)

    def scatter(name, h, value, s_ref, r_ref):
        for b in range(BLKS):
            s_ref[h, b] = value[:, b * BLK : (b + 1) * BLK].astype(BF16)
        plane_push(f"{name}{h}", lambda k, p: s_ref.at[h, p], lambda k, p: r_ref.at[h, k])
        sends.append((f"{name}{h}", r_ref.at[h]))

    def scatter_done(name, h, s_ref, r_ref):
        arrived(r_ref.at[h], f"{name}{h}")
        total = s_ref[h, bk].astype(F32)
        for k in range(BLKS - 1):
            total = total + r_ref[h, k].astype(F32)
        return total

    def gather(name, h, value, v_ref):
        v_ref[h, bk] = value.astype(BF16)
        block = v_ref.at[h, bk]
        plane_push(f"{name}{h}", lambda k, p: block, lambda k, p: block)
        sends.append((f"{name}{h}", v_ref.at[h, pl.ds(0, BLKS - 1)]))

    def gather_done(name, h, v_ref):
        arrived(v_ref.at[h, pl.ds(0, BLKS - 1)], f"{name}{h}")
        return whole(v_ref, h)

    def swap(name, h, src, dst, q):
        rcopy(src, dst, f"{name}{h}", (lf ^ q, bk)).start()
        sends.append((f"{name}{h}", dst))

    local["idx"].wait()
    local["c01"].wait()
    expand0(1, c01)

    local["c02"].wait()
    expand0(2, c02)
    local["c03"].wait()
    expand0(3, c03)

    local["d0"].wait()
    def solve0(name, half):
        arrived(ball0.at[pl.ds(0, BLKS - 1), pl.ds(0, HALF)], name)
        value = dot_nt(jnp.concatenate([ball0[b, pl.ds(half, HALF), :] for b in range(BLKS)], axis=1), d0[...])
        y0r[pl.ds(half, HALF), :] = value
        return value.astype(BF16)

    y0b[...] = solve0("ag0a", other)
    rcopy(y0b, ysib, "y0", sib).start()
    sends.append(("y0", ysib))
    y0c = solve0("ag0b", mine)
    expand0_done(1)
    arrived(ysib, "y0")
    y0c = jnp.concatenate([y0c, ysib[...]], axis=1)
    for h in (0, 1):
        scatter("rsf1", h, dot_nn(rows_of(y0c, h), x0[0]), sf1, rf1)

    spread_done("b1", 1, b1)
    own_rhs(1)
    spread_done("d1", 1, d1)
    permute(1)
    spread("b3", 3, rhs_hbm, STARTS[3], b3)
    spread("d3", 3, d_hbm, STARTS[3], d3)
    spread_done("c12", 1, c12)
    expand_up(1, 2, c12, x12)
    for h in (0, 1):
        total = scatter_done("rsf1", h, sf1, rf1)
        gather("agf1", h, bt[0, part(h), :] - total, vf1)
    for name, ref in (("b2", b2), ("d2", d2), ("c23", c23)):
        forward(name, 2, ref)
    expand0_done(2)
    pend = dot_nn(y0c, x0[1])
    spread_done("c13", 1, c13)
    expand_up(1, 3, c13, x13)
    y1 = []
    for h in (0, 1):
        y1.append(dot_nt(gather_done("agf1", h, vf1), p1[...]))
        scatter("rsf2", h, rows_of(pend, h) + dot_nn(y1[h].astype(BF16), x12[...]), sf2, rf2)
    y1 = both(y1)

    for name, ref in (("b3", b3), ("d3", d3)):
        forward(name, 3, ref)
    spread_done("b2", 2, b2)
    own_rhs(2)
    spread_done("d2", 2, d2)
    permute(2)
    spread_done("c23", 2, c23)
    expand_up(2, 3, c23, x23)
    for h in (0, 1):
        xs[0, h] = scatter_done("rsf2", h, sf2, rf2).astype(BF16)
        swap("xf2", h, xs.at[0, h], xr2.at[h], 2)
    expand0_done(3)
    pend = dot_nn(y0c, x0[2]) + dot_nn(y1.astype(BF16), x13[...])
    for b in range(BLKS):
        sp3[b] = pend[:, b * BLK : (b + 1) * BLK].astype(BF16)
    plane_push("rsp3", lambda k, p: sp3.at[p], lambda k, p: rp3.at[k])
    sends.append(("rsp3", rp3))
    for h in (0, 1):
        arrived(xr2.at[h], f"xf2{h}")
        gather("agf2", h, bt[1, part(h), :] - (xs[0, h].astype(F32) + xr2[h].astype(F32)), vf2)
    spread_done("b3", 3, b3)
    own_rhs(3)
    spread_done("d3", 3, d3)
    permute(3)
    y2 = []
    for h in (0, 1):
        y2.append(dot_nt(gather_done("agf2", h, vf2), p2[...]))
        scatter("rsf3", h, dot_nn(y2[h].astype(BF16), x23[...]), sf3, rf3)

    arrived(rp3, "rsp3")
    total = sp3[bk].astype(F32)
    for k in range(BLKS - 1):
        total = total + rp3[k].astype(F32)
    total = total.astype(BF16)
    xp[...] = total
    for q in (4, 2, 6):
        rcopy(xp, xp3.at[q // 2 - 1], "xp3", (lf ^ q, bk)).start()
    sends.append(("xp3", xp3))
    rest = bt[2, pl.ds(mine, HALF), :] - total.astype(F32)
    arrived(xp3, "xp3")
    for q in range(3):
        rest = rest - xp3[q].astype(F32)
    for h in (0, 1):
        xs[1, h] = scatter_done("rsf3", h, sf3, rf3).astype(BF16)
        swap("xf3", h, xs.at[1, h], xr3.at[h], 6)
    for h in (0, 1):
        arrived(xr3.at[h], f"xf3{h}")
        gather("agf3", h, rows_of(rest, h) - (xs[1, h].astype(F32) + xr3[h].astype(F32)), vf3)

    def keep(level, xo_ref):
        rcopy(xo_ref.at[pl.ds(mine, HALF)], xo_ref.at[pl.ds(mine, HALF)], f"xo{level}", sib).start()
        sends.append((f"xo{level}", xo_ref.at[pl.ds(0, HALF)]))

    def write(level, xo_ref):
        arrived(xo_ref.at[pl.ds(0, HALF)], f"xo{level}")
        count = ROWS[level]
        member = lf & ((1 << level) - 1)
        tmp[...] = xo_ref[...].T
        out[pl.ds(STARTS[level], count), :] = tmp[pl.ds(pl.multiple_of(member * count, count), count), :]

    def down(level, xo_ref, s_ref, r_ref, v_ref):
        for h in (0, 1):
            total = scatter_done(f"rsb{level}", h, s_ref, r_ref)
            gather(f"agb{level}", h, total, v_ref)
            xo_ref[part(h), :] = total
        keep(level, xo_ref)

    for h in (0, 1):
        y3 = dot_nt(gather_done("agf3", h, vf3), p3[...])
        scatter("rsb3", h, dot_nn(y3.astype(BF16), p3[...]), sb3, rb3)
    down(3, xo3, sb3, rb3, vb3)

    for h in (0, 1):
        z = y2[h] - dot_nt(gather_done("agb3", h, vb3), x23[...])
        scatter("rsb2", h, dot_nn(z.astype(BF16), p2[...]), sb2, rb2)
    v = both([whole(vb3, 0), whole(vb3, 1)])
    z1 = y1 - dot_nt(v, x13[...])
    t0 = dot_nt(v, x0[2])
    write(3, xo3)
    down(2, xo2, sb2, rb2, vb2)

    for h in (0, 1):
        z = rows_of(z1, h) - dot_nt(gather_done("agb2", h, vb2), x12[...])
        scatter("rsb1", h, dot_nn(z.astype(BF16), p1[...]), sb1, rb1)
    t0 = t0 + dot_nt(both([whole(vb2, 0), whole(vb2, 1)]), x0[1])
    write(2, xo2)
    down(1, xo1, sb1, rb1, vb1)

    def finish0(name, h, start, z):
        value = dot_nn(z.astype(BF16), d0[...])
        place = pl.ds(pl.multiple_of(start + h * PART, PART), PART)
        for b in range(BLKS):
            s0[b, place, :] = value[:, b * BLK : (b + 1) * BLK].astype(BF16)
        plane_push(f"{name}{h}", lambda k, p: s0.at[p, place], lambda k, p: r0.at[k, place])
        sends.append((f"{name}{h}", r0.at[:, pl.ds(0, PART)]))

    for h in (0, 1):
        t = rows_of(t0, h) + dot_nt(gather_done("agb1", h, vb1), x0[0])
        ssend[h] = t[:, BLK:].astype(BF16)
        swap("sx", h, ssend.at[h], srecv.at[h], 1)
        finish0("rs0a", h, mine, y0r[part(h), :] - t[:, :BLK])
    for h in (0, 1):
        arrived(srecv.at[h], f"sx{h}")
        place = pl.ds(pl.multiple_of(other + h * PART, PART), PART)
        finish0("rs0b", h, other, y0r[place, :] - srecv[h].astype(F32))
    write(1, xo1)
    for name in ("rs0a0", "rs0a1", "rs0b0", "rs0b1"):
        arrived(r0.at[:, pl.ds(0, PART)], name)
    total = s0[bk].astype(F32)
    for k in range(BLKS - 1):
        total = total + r0[k].astype(F32)
    out[pl.ds(0, 128), :] = total.T
    for name, ref in sends:
        rcopy(ref, ref, name, sib).wait_send()


def local(right_side, inverse_blocks, coupling, update_rows):
    def vm(*shape, t=BF16):
        return pltpu.VMEM(shape, t)

    block, part = (HALF, BLK), (PART, BLK)
    scratch = (
        [vm(128, CASES, t=F32), vm(34, UPD, t=jnp.int32)]
        + [vm(128, W)] * 7
        + [vm(128, UPD)] * 6
        + [vm(3, 256, W)]
        + [vm(128, W)] * 3
        + [vm(128, CASES, t=F32)] * 3
        + [vm(3, CASES, BLK, t=F32), vm(BLKS, CASES, BLK)]
        + [vm(CASES, BLK, t=F32), vm(*block), vm(*block)]
        + ([vm(2, BLKS, *part)] * 3 + [vm(2, BLKS - 1, *part)] * 3 + [vm(2, BLKS, *part)] * 3) * 2
        + [vm(2, 2, *part), vm(2, *part), vm(2, *part)]
        + [vm(*block), vm(3, *block), vm(BLKS, *block), vm(BLKS - 1, *block)]
        + [vm(2, *part), vm(2, *part)]
        + [vm(BLKS, CASES, BLK), vm(BLKS - 1, CASES, BLK)]
        + [vm(CASES, BLK, t=F32)] * 3
        + [vm(BLK, CASES, t=F32)]
        + [pltpu.SemaphoreType.DMA((len(NAMES),))] * 2
        + [pltpu.SemaphoreType.DMA((len(LOCALS),))]
    )
    result = pl.pallas_call(
        kernel,
        out_shape=jax.ShapeDtypeStruct((240, CASES), F32),
        in_specs=[pl.BlockSpec(memory_space=pltpu.HBM)] * 4,
        out_specs=pl.BlockSpec(memory_space=pltpu.VMEM),
        scratch_shapes=scratch,
        compiler_params=pltpu.CompilerParams(
            collective_id=0, has_side_effects=True, vmem_limit_bytes=62 * 1024 * 1024
        ),
        name="tree_solve",
    )(right_side[0, 0], inverse_blocks[0, 0], coupling[0, 0], update_rows)
    return result[None, None]


def solution(mesh):
    in_specs = (
        P("leaf", "blk", None, None),
        P("leaf", "blk", None, None),
        P("leaf", "blk", None, None),
        P(),
    )
    out_specs = P("leaf", "blk", None, None)
    return jax.shard_map(local, mesh=mesh, in_specs=in_specs, out_specs=out_specs, check_vma=False)
```

```python
import functools

import jax
import jax.numpy as jnp
from jax import lax
from jax.experimental import pallas as pl
from jax.experimental.pallas import tpu as pltpu
from jax.sharding import PartitionSpec as P

MESH = pl.DeviceIdType.MESH
F32, BF16 = jnp.float32, jnp.bfloat16

W = 2048
UPD = 1024
CASES = 128
HALF = 64
PART = 32
BLKS = 16
BLK = W // BLKS
ROWS = (128, 64, 32, 16)
STARTS = (0, 128, 192, 224)
COUP = {(0, 1): 0, (0, 2): 128, (0, 3): 256, (1, 2): 384, (1, 3): 448, (2, 3): 512}
PAIR_BASE = (0, 24, 32)

NAMES = (
    ["ag0a", "ag0b", "x01", "x02", "x03", "y0"]
    + [f"{name}{way}" for name in ("d1", "c12", "c13", "b1", "d2", "c23", "b2", "d3", "b3") for way in ("", "s")]
    + [f"{name}{l}{h}" for name in ("rsf", "agf", "rsb", "agb") for l in (1, 2, 3) for h in (0, 1)]
    + [f"{name}{h}" for name in ("xf2", "xf3", "sx", "rs0a", "rs0b") for h in (0, 1)]
    + ["rsp3", "xp3", "xo1", "xo2", "xo3"]
)
SEM = {name: i for i, name in enumerate(NAMES)}
LOCALS = ["rhs", "d0", "idx", "c01", "c02", "c03", "d1", "d2", "d3", "c12", "c13", "c23", "b1", "b2", "b3"]
LSEM = {name: i for i, name in enumerate(LOCALS)}


def dot_nt(a, b):
    return lax.dot_general(a, b, (((1,), (1,)), ((), ())), preferred_element_type=F32)


def dot_nn(a, b):
    return jnp.dot(a, b, preferred_element_type=F32)


def far_first(i):
    return jnp.where(i < 2, 2 - i, jnp.where(i == 2, 3, 0))


def kernel(
    rhs_hbm, d_hbm, c_hbm, u_hbm, out,
    rhs0, idx, d0, d1, d2, d3, p1, p2, p3, c01, c02, c03, c12, c13, c23,
    x0, x12, x13, x23, b1, b2, b3, bt, ball0, y0r, y0b, ysib,
    sf1, sf2, sf3, rf1, rf2, rf3, vf1, vf2, vf3,
    sb1, sb2, sb3, rb1, rb2, rb3, vb1, vb2, vb3,
    xs, xr2, xr3, xp, xp3, sp3, rp3, ssend, srecv, s0, r0, xo1, xo2, xo3, tmp,
    ssem, rsem, lsem,
):
    lf, bk = lax.axis_index("leaf"), lax.axis_index("blk")
    core = lax.rem(lf, 2)
    mine = pl.multiple_of(core * HALF, HALF)
    other = pl.multiple_of((1 - core) * HALF, HALF)
    zc, yc = lax.div(bk, 4), lax.rem(bk, 4)
    sib = (lf ^ 1, bk)
    draw, dperm = (d0, d1, d2, d3), (None, p1, p2, p3)
    ball = (None, b1, b2, b3)
    sends = []

    def rcopy(src, dst, name, dev):
        i = SEM[name]
        return pltpu.make_async_remote_copy(
            src_ref=src, dst_ref=dst, send_sem=ssem.at[i], recv_sem=rsem.at[i], device_id=dev, device_id_type=MESH
        )

    def arrived(ref, name):
        rcopy(ref, ref, name, sib).wait_recv()

    def lcopy(src, dst, name):
        return pltpu.make_async_copy(src, dst, lsem.at[LSEM[name]])

    def plane_peer(k):
        z = lax.rem(zc + far_first(lax.div(k, 4)), 4)
        y = lax.rem(yc + far_first(lax.rem(k, 4)), 4)
        return z * 4 + y

    def plane_push(name, src_of, dst_of):
        def body(k, carry):
            p = plane_peer(k)
            rcopy(src_of(k, p), dst_of(k, p), name, (lf, p)).start()
            return carry

        lax.fori_loop(0, BLKS - 1, body, 0)

    local = {}

    def fetch(name, src, dst):
        local[name] = lcopy(src, dst, name)
        local[name].start()

    fetch("rhs", rhs_hbm.at[pl.ds(0, ROWS[0])], rhs0)
    fetch("idx", u_hbm, idx)
    fetch("c01", c_hbm.at[pl.ds(COUP[0, 1], 128)], c01)
    fetch("d0", d_hbm.at[pl.ds(0, 128)], d0)

    barrier = pltpu.get_barrier_semaphore()

    def greet(k, carry):
        pl.semaphore_signal(barrier, inc=1, device_id=(lf, plane_peer(k)), device_id_type=MESH)
        return carry

    lax.fori_loop(0, BLKS - 1, greet, 0)

    def greet_leaf(q, carry):
        pl.semaphore_signal(barrier, inc=1, device_id=(lf ^ q, bk), device_id_type=MESH)
        return carry

    lax.fori_loop(1, 8, greet_leaf, 0)
    local["rhs"].wait()
    ball0[bk] = rhs0[...].T.astype(BF16)
    pl.semaphore_wait(barrier, BLKS - 1 + 7)

    for name, half in (("ag0a", other), ("ag0b", mine)):
        part = ball0.at[bk, pl.ds(half, HALF)]
        plane_push(name, lambda k, p: part, lambda k, p: part)
        sends.append((name, ball0.at[pl.ds(0, BLKS - 1), pl.ds(0, HALF)]))

    def place_of(level, ref, q):
        count = ROWS[level]
        member = (lf ^ q) & ((1 << level) - 1)
        return ref.at[pl.ds(pl.multiple_of(member * count, count), count)]

    def spread(name, level, hbm, start, ref):
        count = ROWS[level]
        src = hbm.at[pl.ds(start, count)]
        for q in range(2, 1 << level, 2):
            rcopy(src, place_of(level, ref, 0), name, (lf ^ q, bk)).start()
        if level == 1:
            rcopy(src, place_of(level, ref, 0), name + "s", sib).start()
            sends.append((name + "s", ref.at[pl.ds(0, count)]))
        else:
            sends.append((name, ref.at[pl.ds(0, BLK // 2 - count)]))
        fetch(name, src, place_of(level, ref, 0))

    def forward(name, level, ref):
        count = ROWS[level]
        local[name].wait()
        arrived(ref.at[pl.ds(0, BLK // 2 - count)], name)
        for q in range(0, 1 << level, 2):
            rcopy(place_of(level, ref, q), place_of(level, ref, q), name + "s", sib).start()
        sends.append((name + "s", ref.at[pl.ds(0, BLK // 2)]))

    def spread_done(name, level, ref):
        if level == 1:
            local[name].wait()
        arrived(ref.at[pl.ds(0, BLK // 2)], name + "s")

    spread("b1", 1, rhs_hbm, STARTS[1], b1)
    spread("d1", 1, d_hbm, STARTS[1], d1)
    fetch("c02", c_hbm.at[pl.ds(COUP[0, 2], 128)], c02)
    fetch("c03", c_hbm.at[pl.ds(COUP[0, 3], 128)], c03)
    spread("c12", 1, c_hbm, COUP[1, 2], c12)
    spread("b2", 2, rhs_hbm, STARTS[2], b2)
    spread("d2", 2, d_hbm, STARTS[2], d2)
    spread("c23", 2, c_hbm, COUP[2, 3], c23)
    spread("c13", 1, c_hbm, COUP[1, 3], c13)

    def expand(c_ref, level, ancestor, store):
        node = lax.div(lf, 1 << level)
        row = PAIR_BASE[level] + node * (3 - level) + (ancestor - level - 1)
        listed = idx[pl.ds(row, 1), :]
        count = ROWS[ancestor]
        bits = count.bit_length() - 1
        place = ((listed >> bits) & (BLKS - 1)) * BLK + (listed >> (bits + 4)) * count + (listed & (count - 1))
        rows = c_ref[...]

        for q in range(W // 256):
            target = lax.broadcasted_iota(jnp.int32, (256, UPD), 0) + q * 256
            hot = jnp.where(target == place, 1.0, 0.0).astype(BF16)
            store(slice(q * 256, (q + 1) * 256), dot_nt(rows, hot).astype(BF16))

    def expand0(ancestor, c_ref):
        a = ancestor - 1

        def store(cols, value):
            x0[a, 0:128, cols] = value

        expand(c_ref, 0, ancestor, store)
        rcopy(x0.at[a, pl.ds(0, 128)], x0.at[a, pl.ds(128, 128)], f"x0{ancestor}", sib).start()
        sends.append((f"x0{ancestor}", x0.at[a, pl.ds(0, 128)]))

    def expand0_done(ancestor):
        arrived(x0.at[ancestor - 1, pl.ds(128, 128)], f"x0{ancestor}")

    def expand_up(level, ancestor, c_ref, x_ref):
        def store(cols, value):
            x_ref[:, cols] = value

        expand(c_ref, level, ancestor, store)

    def permute(level):
        count = ROWS[level]
        lane = lax.broadcasted_iota(jnp.int32, (BLK, BLK), 1)
        for b in range(BLKS):
            total = None
            for m in range(1 << level):
                col = (m * BLKS + b) * count
                tile = draw[level][:, col // BLK * BLK : (col // BLK + 1) * BLK].astype(F32)
                turn = (m * count - col % BLK) % BLK
                if turn:
                    tile = pltpu.roll(tile, turn, 1)
                total = tile if total is None else jnp.where(lane >= m * count, tile, total)
            dperm[level][:, b * BLK : (b + 1) * BLK] = total.astype(BF16)

    def own_rhs(level):
        bt[level - 1] = ball[level][...].T

    def whole(ref, h):
        return jnp.concatenate([ref[h, b] for b in range(BLKS)], axis=1)

    def part(h):
        return pl.ds(pl.multiple_of(mine + h * PART, PART), PART)

    def rows_of(value, h):
        return value[h * PART : (h + 1) * PART]

    def both(values):
        return jnp.concatenate(values, axis=0)

    def scatter(name, h, value, s_ref, r_ref):
        for b in range(BLKS):
            s_ref[h, b] = value[:, b * BLK : (b + 1) * BLK].astype(BF16)
        plane_push(f"{name}{h}", lambda k, p: s_ref.at[h, p], lambda k, p: r_ref.at[h, k])
        sends.append((f"{name}{h}", r_ref.at[h]))

    def scatter_done(name, h, s_ref, r_ref):
        arrived(r_ref.at[h], f"{name}{h}")
        total = s_ref[h, bk].astype(F32)
        for k in range(BLKS - 1):
            total = total + r_ref[h, k].astype(F32)
        return total

    def gather(name, h, value, v_ref):
        v_ref[h, bk] = value.astype(BF16)
        block = v_ref.at[h, bk]
        plane_push(f"{name}{h}", lambda k, p: block, lambda k, p: block)
        sends.append((f"{name}{h}", v_ref.at[h, pl.ds(0, BLKS - 1)]))

    def gather_done(name, h, v_ref):
        arrived(v_ref.at[h, pl.ds(0, BLKS - 1)], f"{name}{h}")
        return whole(v_ref, h)

    def swap(name, h, src, dst, q):
        rcopy(src, dst, f"{name}{h}", (lf ^ q, bk)).start()
        sends.append((f"{name}{h}", dst))

    local["idx"].wait()
    local["c01"].wait()
    expand0(1, c01)

    local["d0"].wait()
    def solve0(name, half):
        arrived(ball0.at[pl.ds(0, BLKS - 1), pl.ds(0, HALF)], name)
        value = dot_nt(jnp.concatenate([ball0[b, pl.ds(half, HALF), :] for b in range(BLKS)], axis=1), d0[...])
        y0r[pl.ds(half, HALF), :] = value
        return value.astype(BF16)

    y0b[...] = solve0("ag0a", other)
    rcopy(y0b, ysib, "y0", sib).start()
    sends.append(("y0", ysib))
    y0c = solve0("ag0b", mine)
    expand0_done(1)
    arrived(ysib, "y0")
    y0c = jnp.concatenate([y0c, ysib[...]], axis=1)
    for h in (0, 1):
        scatter("rsf1", h, dot_nn(rows_of(y0c, h), x0[0]), sf1, rf1)

    spread_done("b1", 1, b1)
    own_rhs(1)
    spread_done("d1", 1, d1)
    permute(1)
    spread("b3", 3, rhs_hbm, STARTS[3], b3)
    spread("d3", 3, d_hbm, STARTS[3], d3)
    local["c02"].wait()
    expand0(2, c02)
    for h in (0, 1):
        total = scatter_done("rsf1", h, sf1, rf1)
        gather("agf1", h, bt[0, part(h), :] - total, vf1)
    for name, ref in (("b2", b2), ("d2", d2), ("c23", c23)):
        forward(name, 2, ref)
    spread_done("c12", 1, c12)
    expand_up(1, 2, c12, x12)
    expand0_done(2)
    pend = dot_nn(y0c, x0[1])
    y1 = []
    for h in (0, 1):
        y1.append(dot_nt(gather_done("agf1", h, vf1), p1[...]))
        scatter("rsf2", h, rows_of(pend, h) + dot_nn(y1[h].astype(BF16), x12[...]), sf2, rf2)
    y1 = both(y1)

    for name, ref in (("b3", b3), ("d3", d3)):
        forward(name, 3, ref)
    spread_done("b2", 2, b2)
    own_rhs(2)
    spread_done("d2", 2, d2)
    permute(2)
    local["c03"].wait()
    expand0(3, c03)
    for h in (0, 1):
        xs[0, h] = scatter_done("rsf2", h, sf2, rf2).astype(BF16)
        swap("xf2", h, xs.at[0, h], xr2.at[h], 2)
    spread_done("c13", 1, c13)
    expand_up(1, 3, c13, x13)
    expand0_done(3)
    pend = dot_nn(y0c, x0[2]) + dot_nn(y1.astype(BF16), x13[...])
    for b in range(BLKS):
        sp3[b] = pend[:, b * BLK : (b + 1) * BLK].astype(BF16)
    plane_push("rsp3", lambda k, p: sp3.at[p], lambda k, p: rp3.at[k])
    sends.append(("rsp3", rp3))
    for h in (0, 1):
        arrived(xr2.at[h], f"xf2{h}")
        gather("agf2", h, bt[1, part(h), :] - (xs[0, h].astype(F32) + xr2[h].astype(F32)), vf2)
    spread_done("c23", 2, c23)
    expand_up(2, 3, c23, x23)
    y2 = []
    for h in (0, 1):
        y2.append(dot_nt(gather_done("agf2", h, vf2), p2[...]))
        scatter("rsf3", h, dot_nn(y2[h].astype(BF16), x23[...]), sf3, rf3)

    arrived(rp3, "rsp3")
    total = sp3[bk].astype(F32)
    for k in range(BLKS - 1):
        total = total + rp3[k].astype(F32)
    total = total.astype(BF16)
    xp[...] = total
    for q in (4, 2, 6):
        rcopy(xp, xp3.at[q // 2 - 1], "xp3", (lf ^ q, bk)).start()
    sends.append(("xp3", xp3))
    spread_done("b3", 3, b3)
    own_rhs(3)
    spread_done("d3", 3, d3)
    permute(3)
    rest = bt[2, pl.ds(mine, HALF), :] - total.astype(F32)
    arrived(xp3, "xp3")
    for q in range(3):
        rest = rest - xp3[q].astype(F32)
    for h in (0, 1):
        xs[1, h] = scatter_done("rsf3", h, sf3, rf3).astype(BF16)
        swap("xf3", h, xs.at[1, h], xr3.at[h], 6)
    for h in (0, 1):
        arrived(xr3.at[h], f"xf3{h}")
        gather("agf3", h, rows_of(rest, h) - (xs[1, h].astype(F32) + xr3[h].astype(F32)), vf3)

    def keep(level, xo_ref):
        rcopy(xo_ref.at[pl.ds(mine, HALF)], xo_ref.at[pl.ds(mine, HALF)], f"xo{level}", sib).start()
        sends.append((f"xo{level}", xo_ref.at[pl.ds(0, HALF)]))

    def write(level, xo_ref):
        arrived(xo_ref.at[pl.ds(0, HALF)], f"xo{level}")
        count = ROWS[level]
        member = lf & ((1 << level) - 1)
        tmp[...] = xo_ref[...].T
        out[pl.ds(STARTS[level], count), :] = tmp[pl.ds(pl.multiple_of(member * count, count), count), :]

    def down(level, xo_ref, s_ref, r_ref, v_ref):
        for h in (0, 1):
            total = scatter_done(f"rsb{level}", h, s_ref, r_ref)
            gather(f"agb{level}", h, total, v_ref)
            xo_ref[part(h), :] = total
        keep(level, xo_ref)

    for h in (0, 1):
        y3 = dot_nt(gather_done("agf3", h, vf3), p3[...])
        scatter("rsb3", h, dot_nn(y3.astype(BF16), p3[...]), sb3, rb3)
    down(3, xo3, sb3, rb3, vb3)

    for h in (0, 1):
        z = y2[h] - dot_nt(gather_done("agb3", h, vb3), x23[...])
        scatter("rsb2", h, dot_nn(z.astype(BF16), p2[...]), sb2, rb2)
    v = both([whole(vb3, 0), whole(vb3, 1)])
    z1 = y1 - dot_nt(v, x13[...])
    t0 = dot_nt(v, x0[2])
    write(3, xo3)
    down(2, xo2, sb2, rb2, vb2)

    for h in (0, 1):
        z = rows_of(z1, h) - dot_nt(gather_done("agb2", h, vb2), x12[...])
        scatter("rsb1", h, dot_nn(z.astype(BF16), p1[...]), sb1, rb1)
    t0 = t0 + dot_nt(both([whole(vb2, 0), whole(vb2, 1)]), x0[1])
    write(2, xo2)
    down(1, xo1, sb1, rb1, vb1)

    def finish0(name, h, start, z):
        value = dot_nn(z.astype(BF16), d0[...])
        place = pl.ds(pl.multiple_of(start + h * PART, PART), PART)
        for b in range(BLKS):
            s0[b, place, :] = value[:, b * BLK : (b + 1) * BLK].astype(BF16)
        plane_push(f"{name}{h}", lambda k, p: s0.at[p, place], lambda k, p: r0.at[k, place])
        sends.append((f"{name}{h}", r0.at[:, pl.ds(0, PART)]))

    for h in (0, 1):
        t = rows_of(t0, h) + dot_nt(gather_done("agb1", h, vb1), x0[0])
        ssend[h] = t[:, BLK:].astype(BF16)
        swap("sx", h, ssend.at[h], srecv.at[h], 1)
        finish0("rs0a", h, mine, y0r[part(h), :] - t[:, :BLK])
    for h in (0, 1):
        arrived(srecv.at[h], f"sx{h}")
        place = pl.ds(pl.multiple_of(other + h * PART, PART), PART)
        finish0("rs0b", h, other, y0r[place, :] - srecv[h].astype(F32))
    write(1, xo1)
    for name in ("rs0a0", "rs0a1", "rs0b0", "rs0b1"):
        arrived(r0.at[:, pl.ds(0, PART)], name)
    total = s0[bk].astype(F32)
    for k in range(BLKS - 1):
        total = total + r0[k].astype(F32)
    out[pl.ds(0, 128), :] = total.T
    for name, ref in sends:
        rcopy(ref, ref, name, sib).wait_send()


def local(right_side, inverse_blocks, coupling, update_rows):
    def vm(*shape, t=BF16):
        return pltpu.VMEM(shape, t)

    block, part = (HALF, BLK), (PART, BLK)
    scratch = (
        [vm(128, CASES, t=F32), vm(34, UPD, t=jnp.int32)]
        + [vm(128, W)] * 7
        + [vm(128, UPD)] * 6
        + [vm(3, 256, W)]
        + [vm(128, W)] * 3
        + [vm(128, CASES, t=F32)] * 3
        + [vm(3, CASES, BLK, t=F32), vm(BLKS, CASES, BLK)]
        + [vm(CASES, BLK, t=F32), vm(*block), vm(*block)]
        + ([vm(2, BLKS, *part)] * 3 + [vm(2, BLKS - 1, *part)] * 3 + [vm(2, BLKS, *part)] * 3) * 2
        + [vm(2, 2, *part), vm(2, *part), vm(2, *part)]
        + [vm(*block), vm(3, *block), vm(BLKS, *block), vm(BLKS - 1, *block)]
        + [vm(2, *part), vm(2, *part)]
        + [vm(BLKS, CASES, BLK), vm(BLKS - 1, CASES, BLK)]
        + [vm(CASES, BLK, t=F32)] * 3
        + [vm(BLK, CASES, t=F32)]
        + [pltpu.SemaphoreType.DMA((len(NAMES),))] * 2
        + [pltpu.SemaphoreType.DMA((len(LOCALS),))]
    )
    result = pl.pallas_call(
        kernel,
        out_shape=jax.ShapeDtypeStruct((240, CASES), F32),
        in_specs=[pl.BlockSpec(memory_space=pltpu.HBM)] * 4,
        out_specs=pl.BlockSpec(memory_space=pltpu.VMEM),
        scratch_shapes=scratch,
        compiler_params=pltpu.CompilerParams(
            collective_id=0, has_side_effects=True, vmem_limit_bytes=56413184
        ),
        name="tree_solve",
    )(right_side[0, 0], inverse_blocks[0, 0], coupling[0, 0], update_rows)
    return result[None, None]


def solution(mesh):
    in_specs = (
        P("leaf", "blk", None, None),
        P("leaf", "blk", None, None),
        P("leaf", "blk", None, None),
        P(),
    )
    out_specs = P("leaf", "blk", None, None)
    return jax.shard_map(local, mesh=mesh, in_specs=in_specs, out_specs=out_specs, check_vma=False)
```

```python
import functools

import jax
import jax.numpy as jnp
from jax import lax
from jax.experimental import pallas as pl
from jax.experimental.pallas import tpu as pltpu
from jax.sharding import PartitionSpec as P

MESH = pl.DeviceIdType.MESH
F32, BF16 = jnp.float32, jnp.bfloat16

W = 2048
UPD = 1024
CASES = 128
HALF = 64
PART = 32
BLKS = 16
BLK = W // BLKS
ROWS = (128, 64, 32, 16)
STARTS = (0, 128, 192, 224)
COUP = {(0, 1): 0, (0, 2): 128, (0, 3): 256, (1, 2): 384, (1, 3): 448, (2, 3): 512}
PAIR_BASE = (0, 24, 32)

NAMES = (
    ["ag0a", "ag0b", "x01", "x02", "x03", "y0"]
    + [f"{name}{way}" for name in ("d1", "c12", "c13", "b1", "d2", "c23", "b2", "d3", "b3") for way in ("", "s")]
    + [f"{name}{l}{h}" for name in ("rsf", "agf", "rsb", "agb") for l in (1, 2, 3) for h in (0, 1)]
    + [f"{name}{h}" for name in ("xf2", "xf3", "sx", "rs0a", "rs0b") for h in (0, 1)]
    + ["rsp3", "xp3", "xo1", "xo2", "xo3"]
)
SEM = {name: i for i, name in enumerate(NAMES)}
LOCALS = ["rhs", "d0", "idx", "c01", "c02", "c03", "d1", "d2", "d3", "c12", "c13", "c23", "b1", "b2", "b3"]
LSEM = {name: i for i, name in enumerate(LOCALS)}


def dot_nt(a, b):
    return lax.dot_general(a, b, (((1,), (1,)), ((), ())), preferred_element_type=F32)


def dot_nn(a, b):
    return jnp.dot(a, b, preferred_element_type=F32)


def far_first(i):
    return jnp.where(i < 2, 2 - i, jnp.where(i == 2, 3, 0))


def kernel(
    rhs_hbm, d_hbm, c_hbm, u_hbm, out,
    rhs0, idx, d0, d1, d2, d3, p1, p2, p3, c01, c02, c03, c12, c13, c23,
    x0, x12, x13, x23, b1, b2, b3, bt, ball0, y0r, y0b, ysib,
    sf1, sf2, sf3, rf1, rf2, rf3, vf1, vf2, vf3,
    sb1, sb2, sb3, rb1, rb2, rb3, vb1, vb2, vb3,
    xs, xr2, xr3, xp, xp3, sp3, rp3, ssend, srecv, s0, r0, xo1, xo2, xo3, tmp,
    ssem, rsem, lsem,
):
    lf, bk = lax.axis_index("leaf"), lax.axis_index("blk")
    core = lax.rem(lf, 2)
    mine = pl.multiple_of(core * HALF, HALF)
    other = pl.multiple_of((1 - core) * HALF, HALF)
    zc, yc = lax.div(bk, 4), lax.rem(bk, 4)
    sib = (lf ^ 1, bk)
    draw, dperm = (d0, d1, d2, d3), (None, p1, p2, p3)
    ball = (None, b1, b2, b3)
    sends = []

    def rcopy(src, dst, name, dev):
        i = SEM[name]
        return pltpu.make_async_remote_copy(
            src_ref=src, dst_ref=dst, send_sem=ssem.at[i], recv_sem=rsem.at[i], device_id=dev, device_id_type=MESH
        )

    def arrived(ref, name):
        rcopy(ref, ref, name, sib).wait_recv()

    def lcopy(src, dst, name):
        return pltpu.make_async_copy(src, dst, lsem.at[LSEM[name]])

    def plane_peer(k):
        z = lax.rem(zc + far_first(lax.div(k, 4)), 4)
        y = lax.rem(yc + far_first(lax.rem(k, 4)), 4)
        return z * 4 + y

    def plane_push(name, src_of, dst_of):
        def body(k, carry):
            p = plane_peer(k)
            rcopy(src_of(k, p), dst_of(k, p), name, (lf, p)).start()
            return carry

        lax.fori_loop(0, BLKS - 1, body, 0)

    local = {}

    def fetch(name, src, dst):
        local[name] = lcopy(src, dst, name)
        local[name].start()

    fetch("rhs", rhs_hbm.at[pl.ds(0, ROWS[0])], rhs0)
    fetch("idx", u_hbm, idx)
    fetch("c01", c_hbm.at[pl.ds(COUP[0, 1], 128)], c01)
    fetch("d0", d_hbm.at[pl.ds(0, 128)], d0)

    barrier = pltpu.get_barrier_semaphore()

    def greet(k, carry):
        pl.semaphore_signal(barrier, inc=1, device_id=(lf, plane_peer(k)), device_id_type=MESH)
        return carry

    lax.fori_loop(0, BLKS - 1, greet, 0)

    def greet_leaf(q, carry):
        pl.semaphore_signal(barrier, inc=1, device_id=(lf ^ q, bk), device_id_type=MESH)
        return carry

    lax.fori_loop(1, 8, greet_leaf, 0)
    local["rhs"].wait()
    ball0[bk] = rhs0[...].T.astype(BF16)
    pl.semaphore_wait(barrier, BLKS - 1 + 7)

    for name, half in (("ag0a", other), ("ag0b", mine)):
        part = ball0.at[bk, pl.ds(half, HALF)]
        plane_push(name, lambda k, p: part, lambda k, p: part)
        sends.append((name, ball0.at[pl.ds(0, BLKS - 1), pl.ds(0, HALF)]))

    def place_of(level, ref, q):
        count = ROWS[level]
        member = (lf ^ q) & ((1 << level) - 1)
        return ref.at[pl.ds(pl.multiple_of(member * count, count), count)]

    def spread(name, level, hbm, start, ref):
        count = ROWS[level]
        src = hbm.at[pl.ds(start, count)]
        for q in range(2, 1 << level, 2):
            rcopy(src, place_of(level, ref, 0), name, (lf ^ q, bk)).start()
        if level == 1:
            rcopy(src, place_of(level, ref, 0), name + "s", sib).start()
            sends.append((name + "s", ref.at[pl.ds(0, count)]))
        else:
            sends.append((name, ref.at[pl.ds(0, BLK // 2 - count)]))
        fetch(name, src, place_of(level, ref, 0))

    def forward(name, level, ref):
        count = ROWS[level]
        local[name].wait()
        arrived(ref.at[pl.ds(0, BLK // 2 - count)], name)
        for q in range(0, 1 << level, 2):
            rcopy(place_of(level, ref, q), place_of(level, ref, q), name + "s", sib).start()
        sends.append((name + "s", ref.at[pl.ds(0, BLK // 2)]))

    def spread_done(name, level, ref):
        if level == 1:
            local[name].wait()
        arrived(ref.at[pl.ds(0, BLK // 2)], name + "s")

    spread("b1", 1, rhs_hbm, STARTS[1], b1)
    spread("d1", 1, d_hbm, STARTS[1], d1)
    fetch("c02", c_hbm.at[pl.ds(COUP[0, 2], 128)], c02)
    fetch("c03", c_hbm.at[pl.ds(COUP[0, 3], 128)], c03)
    spread("c12", 1, c_hbm, COUP[1, 2], c12)
    spread("b2", 2, rhs_hbm, STARTS[2], b2)
    spread("d2", 2, d_hbm, STARTS[2], d2)
    spread("c23", 2, c_hbm, COUP[2, 3], c23)
    spread("c13", 1, c_hbm, COUP[1, 3], c13)

    def expand(c_ref, level, ancestor, store):
        node = lax.div(lf, 1 << level)
        row = PAIR_BASE[level] + node * (3 - level) + (ancestor - level - 1)
        listed = idx[pl.ds(row, 1), :]
        count = ROWS[ancestor]
        bits = count.bit_length() - 1
        place = ((listed >> bits) & (BLKS - 1)) * BLK + (listed >> (bits + 4)) * count + (listed & (count - 1))
        rows = c_ref[...]

        for q in range(W // 256):
            target = lax.broadcasted_iota(jnp.int32, (256, UPD), 0) + q * 256
            hot = jnp.where(target == place, 1.0, 0.0).astype(BF16)
            store(slice(q * 256, (q + 1) * 256), dot_nt(rows, hot).astype(BF16))

    def expand0(ancestor, c_ref):
        a = ancestor - 1

        def store(cols, value):
            x0[a, 0:128, cols] = value

        expand(c_ref, 0, ancestor, store)
        rcopy(x0.at[a, pl.ds(0, 128)], x0.at[a, pl.ds(128, 128)], f"x0{ancestor}", sib).start()
        sends.append((f"x0{ancestor}", x0.at[a, pl.ds(0, 128)]))

    def expand0_done(ancestor):
        arrived(x0.at[ancestor - 1, pl.ds(128, 128)], f"x0{ancestor}")

    def expand_up(level, ancestor, c_ref, x_ref):
        def store(cols, value):
            x_ref[:, cols] = value

        expand(c_ref, level, ancestor, store)

    def permute(level):
        count = ROWS[level]
        lane = lax.broadcasted_iota(jnp.int32, (BLK, BLK), 1)
        for b in range(BLKS):
            total = None
            for m in range(1 << level):
                col = (m * BLKS + b) * count
                tile = draw[level][:, col // BLK * BLK : (col // BLK + 1) * BLK].astype(F32)
                turn = (m * count - col % BLK) % BLK
                if turn:
                    tile = pltpu.roll(tile, turn, 1)
                total = tile if total is None else jnp.where(lane >= m * count, tile, total)
            dperm[level][:, b * BLK : (b + 1) * BLK] = total.astype(BF16)

    def own_rhs(level):
        bt[level - 1] = ball[level][...].T

    def whole(ref, h):
        return jnp.concatenate([ref[h, b] for b in range(BLKS)], axis=1)

    def part(h):
        return pl.ds(pl.multiple_of(mine + h * PART, PART), PART)

    def rows_of(value, h):
        return value[h * PART : (h + 1) * PART]

    def both(values):
        return jnp.concatenate(values, axis=0)

    def scatter(name, h, value, s_ref, r_ref):
        for b in range(BLKS):
            s_ref[h, b] = value[:, b * BLK : (b + 1) * BLK].astype(BF16)
        plane_push(f"{name}{h}", lambda k, p: s_ref.at[h, p], lambda k, p: r_ref.at[h, k])
        sends.append((f"{name}{h}", r_ref.at[h]))

    def scatter_done(name, h, s_ref, r_ref):
        arrived(r_ref.at[h], f"{name}{h}")
        total = s_ref[h, bk].astype(F32)
        for k in range(BLKS - 1):
            total = total + r_ref[h, k].astype(F32)
        return total

    def gather(name, h, value, v_ref):
        v_ref[h, bk] = value.astype(BF16)
        block = v_ref.at[h, bk]
        plane_push(f"{name}{h}", lambda k, p: block, lambda k, p: block)
        sends.append((f"{name}{h}", v_ref.at[h, pl.ds(0, BLKS - 1)]))

    def gather_done(name, h, v_ref):
        arrived(v_ref.at[h, pl.ds(0, BLKS - 1)], f"{name}{h}")
        return whole(v_ref, h)

    def swap(name, h, src, dst, q):
        rcopy(src, dst, f"{name}{h}", (lf ^ q, bk)).start()
        sends.append((f"{name}{h}", dst))

    local["idx"].wait()
    local["c01"].wait()
    expand0(1, c01)

    local["d0"].wait()
    def solve0(name, half):
        arrived(ball0.at[pl.ds(0, BLKS - 1), pl.ds(0, HALF)], name)
        value = dot_nt(jnp.concatenate([ball0[b, pl.ds(half, HALF), :] for b in range(BLKS)], axis=1), d0[...])
        y0r[pl.ds(half, HALF), :] = value
        return value.astype(BF16)

    y0b[...] = solve0("ag0a", other)
    rcopy(y0b, ysib, "y0", sib).start()
    sends.append(("y0", ysib))
    local["c02"].wait()
    expand0(2, c02)
    y0c = solve0("ag0b", mine)
    expand0_done(1)
    arrived(ysib, "y0")
    y0c = jnp.concatenate([y0c, ysib[...]], axis=1)
    for h in (0, 1):
        scatter("rsf1", h, dot_nn(rows_of(y0c, h), x0[0]), sf1, rf1)

    spread_done("b1", 1, b1)
    own_rhs(1)
    spread_done("d1", 1, d1)
    permute(1)
    spread("b3", 3, rhs_hbm, STARTS[3], b3)
    spread("d3", 3, d_hbm, STARTS[3], d3)
    spread_done("c12", 1, c12)
    expand_up(1, 2, c12, x12)
    for h in (0, 1):
        total = scatter_done("rsf1", h, sf1, rf1)
        gather("agf1", h, bt[0, part(h), :] - total, vf1)
    for name, ref in (("b2", b2), ("d2", d2), ("c23", c23)):
        forward(name, 2, ref)
    local["c03"].wait()
    expand0(3, c03)
    expand0_done(2)
    pend = dot_nn(y0c, x0[1])
    y1 = []
    for h in (0, 1):
        y1.append(dot_nt(gather_done("agf1", h, vf1), p1[...]))
        scatter("rsf2", h, rows_of(pend, h) + dot_nn(y1[h].astype(BF16), x12[...]), sf2, rf2)
    y1 = both(y1)

    for name, ref in (("b3", b3), ("d3", d3)):
        forward(name, 3, ref)
    spread_done("b2", 2, b2)
    own_rhs(2)
    spread_done("d2", 2, d2)
    permute(2)
    spread_done("c13", 1, c13)
    expand_up(1, 3, c13, x13)
    for h in (0, 1):
        xs[0, h] = scatter_done("rsf2", h, sf2, rf2).astype(BF16)
        swap("xf2", h, xs.at[0, h], xr2.at[h], 2)
    expand0_done(3)
    pend = dot_nn(y0c, x0[2]) + dot_nn(y1.astype(BF16), x13[...])
    for b in range(BLKS):
        sp3[b] = pend[:, b * BLK : (b + 1) * BLK].astype(BF16)
    plane_push("rsp3", lambda k, p: sp3.at[p], lambda k, p: rp3.at[k])
    sends.append(("rsp3", rp3))
    for h in (0, 1):
        arrived(xr2.at[h], f"xf2{h}")
        gather("agf2", h, bt[1, part(h), :] - (xs[0, h].astype(F32) + xr2[h].astype(F32)), vf2)
    spread_done("c23", 2, c23)
    expand_up(2, 3, c23, x23)
    y2 = []
    for h in (0, 1):
        y2.append(dot_nt(gather_done("agf2", h, vf2), p2[...]))
        scatter("rsf3", h, dot_nn(y2[h].astype(BF16), x23[...]), sf3, rf3)

    arrived(rp3, "rsp3")
    total = sp3[bk].astype(F32)
    for k in range(BLKS - 1):
        total = total + rp3[k].astype(F32)
    total = total.astype(BF16)
    xp[...] = total
    for q in (4, 2, 6):
        rcopy(xp, xp3.at[q // 2 - 1], "xp3", (lf ^ q, bk)).start()
    sends.append(("xp3", xp3))
    spread_done("b3", 3, b3)
    own_rhs(3)
    spread_done("d3", 3, d3)
    permute(3)
    rest = bt[2, pl.ds(mine, HALF), :] - total.astype(F32)
    arrived(xp3, "xp3")
    for q in range(3):
        rest = rest - xp3[q].astype(F32)
    for h in (0, 1):
        xs[1, h] = scatter_done("rsf3", h, sf3, rf3).astype(BF16)
        swap("xf3", h, xs.at[1, h], xr3.at[h], 6)
    for h in (0, 1):
        arrived(xr3.at[h], f"xf3{h}")
        gather("agf3", h, rows_of(rest, h) - (xs[1, h].astype(F32) + xr3[h].astype(F32)), vf3)

    def keep(level, xo_ref):
        rcopy(xo_ref.at[pl.ds(mine, HALF)], xo_ref.at[pl.ds(mine, HALF)], f"xo{level}", sib).start()
        sends.append((f"xo{level}", xo_ref.at[pl.ds(0, HALF)]))

    def write(level, xo_ref):
        arrived(xo_ref.at[pl.ds(0, HALF)], f"xo{level}")
        count = ROWS[level]
        member = lf & ((1 << level) - 1)
        tmp[...] = xo_ref[...].T
        out[pl.ds(STARTS[level], count), :] = tmp[pl.ds(pl.multiple_of(member * count, count), count), :]

    def down(level, xo_ref, s_ref, r_ref, v_ref):
        for h in (0, 1):
            total = scatter_done(f"rsb{level}", h, s_ref, r_ref)
            gather(f"agb{level}", h, total, v_ref)
            xo_ref[part(h), :] = total
        keep(level, xo_ref)

    for h in (0, 1):
        y3 = dot_nt(gather_done("agf3", h, vf3), p3[...])
        scatter("rsb3", h, dot_nn(y3.astype(BF16), p3[...]), sb3, rb3)
    down(3, xo3, sb3, rb3, vb3)

    for h in (0, 1):
        z = y2[h] - dot_nt(gather_done("agb3", h, vb3), x23[...])
        scatter("rsb2", h, dot_nn(z.astype(BF16), p2[...]), sb2, rb2)
    v = both([whole(vb3, 0), whole(vb3, 1)])
    z1 = y1 - dot_nt(v, x13[...])
    t0 = dot_nt(v, x0[2])
    write(3, xo3)
    down(2, xo2, sb2, rb2, vb2)

    for h in (0, 1):
        z = rows_of(z1, h) - dot_nt(gather_done("agb2", h, vb2), x12[...])
        scatter("rsb1", h, dot_nn(z.astype(BF16), p1[...]), sb1, rb1)
    t0 = t0 + dot_nt(both([whole(vb2, 0), whole(vb2, 1)]), x0[1])
    write(2, xo2)
    down(1, xo1, sb1, rb1, vb1)

    def finish0(name, h, start, z):
        value = dot_nn(z.astype(BF16), d0[...])
        place = pl.ds(pl.multiple_of(start + h * PART, PART), PART)
        for b in range(BLKS):
            s0[b, place, :] = value[:, b * BLK : (b + 1) * BLK].astype(BF16)
        plane_push(f"{name}{h}", lambda k, p: s0.at[p, place], lambda k, p: r0.at[k, place])
        sends.append((f"{name}{h}", r0.at[:, pl.ds(0, PART)]))

    for h in (0, 1):
        t = rows_of(t0, h) + dot_nt(gather_done("agb1", h, vb1), x0[0])
        ssend[h] = t[:, BLK:].astype(BF16)
        swap("sx", h, ssend.at[h], srecv.at[h], 1)
        finish0("rs0a", h, mine, y0r[part(h), :] - t[:, :BLK])
    for h in (0, 1):
        arrived(srecv.at[h], f"sx{h}")
        place = pl.ds(pl.multiple_of(other + h * PART, PART), PART)
        finish0("rs0b", h, other, y0r[place, :] - srecv[h].astype(F32))
    write(1, xo1)
    for name in ("rs0a0", "rs0a1", "rs0b0", "rs0b1"):
        arrived(r0.at[:, pl.ds(0, PART)], name)
    total = s0[bk].astype(F32)
    for k in range(BLKS - 1):
        total = total + r0[k].astype(F32)
    out[pl.ds(0, 128), :] = total.T
    for name, ref in sends:
        rcopy(ref, ref, name, sib).wait_send()


def local(right_side, inverse_blocks, coupling, update_rows):
    def vm(*shape, t=BF16):
        return pltpu.VMEM(shape, t)

    block, part = (HALF, BLK), (PART, BLK)
    scratch = (
        [vm(128, CASES, t=F32), vm(34, UPD, t=jnp.int32)]
        + [vm(128, W)] * 7
        + [vm(128, UPD)] * 6
        + [vm(3, 256, W)]
        + [vm(128, W)] * 3
        + [vm(128, CASES, t=F32)] * 3
        + [vm(3, CASES, BLK, t=F32), vm(BLKS, CASES, BLK)]
        + [vm(CASES, BLK, t=F32), vm(*block), vm(*block)]
        + ([vm(2, BLKS, *part)] * 3 + [vm(2, BLKS - 1, *part)] * 3 + [vm(2, BLKS, *part)] * 3) * 2
        + [vm(2, 2, *part), vm(2, *part), vm(2, *part)]
        + [vm(*block), vm(3, *block), vm(BLKS, *block), vm(BLKS - 1, *block)]
        + [vm(2, *part), vm(2, *part)]
        + [vm(BLKS, CASES, BLK), vm(BLKS - 1, CASES, BLK)]
        + [vm(CASES, BLK, t=F32)] * 3
        + [vm(BLK, CASES, t=F32)]
        + [pltpu.SemaphoreType.DMA((len(NAMES),))] * 2
        + [pltpu.SemaphoreType.DMA((len(LOCALS),))]
    )
    result = pl.pallas_call(
        kernel,
        out_shape=jax.ShapeDtypeStruct((240, CASES), F32),
        in_specs=[pl.BlockSpec(memory_space=pltpu.HBM)] * 4,
        out_specs=pl.BlockSpec(memory_space=pltpu.VMEM),
        scratch_shapes=scratch,
        compiler_params=pltpu.CompilerParams(
            collective_id=0, has_side_effects=True, vmem_limit_bytes=56413184
        ),
        name="tree_solve",
    )(right_side[0, 0], inverse_blocks[0, 0], coupling[0, 0], update_rows)
    return result[None, None]


def solution(mesh):
    in_specs = (
        P("leaf", "blk", None, None),
        P("leaf", "blk", None, None),
        P("leaf", "blk", None, None),
        P(),
    )
    out_specs = P("leaf", "blk", None, None)
    return jax.shard_map(local, mesh=mesh, in_specs=in_specs, out_specs=out_specs, check_vma=False)
```

```python
import functools

import jax
import jax.numpy as jnp
from jax import lax
from jax.experimental import pallas as pl
from jax.experimental.pallas import tpu as pltpu
from jax.sharding import PartitionSpec as P

MESH = pl.DeviceIdType.MESH
F32, BF16 = jnp.float32, jnp.bfloat16

W = 2048
UPD = 1024
CASES = 128
HALF = 64
PART = 32
BLKS = 16
BLK = W // BLKS
ROWS = (128, 64, 32, 16)
STARTS = (0, 128, 192, 224)
COUP = {(0, 1): 0, (0, 2): 128, (0, 3): 256, (1, 2): 384, (1, 3): 448, (2, 3): 512}
PAIR_BASE = (0, 24, 32)

NAMES = (
    ["ag0a", "ag0b", "x01", "x02", "x03", "y0"]
    + [f"{name}{way}" for name in ("d1", "c12", "c13", "b1", "d2", "c23", "b2", "d3", "b3") for way in ("", "s")]
    + [f"{name}{l}{h}" for name in ("rsf", "agf", "rsb", "agb") for l in (1, 2, 3) for h in (0, 1)]
    + [f"{name}{h}" for name in ("xf2", "xf3", "sx", "rs0a", "rs0b") for h in (0, 1)]
    + ["rsp3", "xp3", "xo1", "xo2", "xo3"]
)
SEM = {name: i for i, name in enumerate(NAMES)}
LOCALS = ["rhs", "d0", "idx", "c01", "c02", "c03", "d1", "d2", "d3", "c12", "c13", "c23", "b1", "b2", "b3"]
LSEM = {name: i for i, name in enumerate(LOCALS)}


def dot_nt(a, b):
    return lax.dot_general(a, b, (((1,), (1,)), ((), ())), preferred_element_type=F32)


def dot_nn(a, b):
    return jnp.dot(a, b, preferred_element_type=F32)


def far_first(i):
    return jnp.where(i < 2, 2 - i, jnp.where(i == 2, 3, 0))


def kernel(
    rhs_hbm, d_hbm, c_hbm, u_hbm, out,
    rhs0, idx, d0, d1, d2, d3, p1, p2, p3, c01, c02, c03, c12, c13, c23,
    x0, x12, x13, x23, b1, b2, b3, bt, ball0, y0r, y0b, ysib,
    sf1, sf2, sf3, rf1, rf2, rf3, vf1, vf2, vf3,
    sb1, sb2, sb3, rb1, rb2, rb3, vb1, vb2, vb3,
    xs, xr2, xr3, xp, xp3, sp3, rp3, ssend, srecv, s0, r0, xo1, xo2, xo3, tmp,
    ssem, rsem, lsem,
):
    lf, bk = lax.axis_index("leaf"), lax.axis_index("blk")
    core = lax.rem(lf, 2)
    mine = pl.multiple_of(core * HALF, HALF)
    other = pl.multiple_of((1 - core) * HALF, HALF)
    zc, yc = lax.div(bk, 4), lax.rem(bk, 4)
    sib = (lf ^ 1, bk)
    draw, dperm = (d0, d1, d2, d3), (None, p1, p2, p3)
    ball = (None, b1, b2, b3)
    sends = []

    def rcopy(src, dst, name, dev):
        i = SEM[name]
        return pltpu.make_async_remote_copy(
            src_ref=src, dst_ref=dst, send_sem=ssem.at[i], recv_sem=rsem.at[i], device_id=dev, device_id_type=MESH
        )

    def arrived(ref, name):
        rcopy(ref, ref, name, sib).wait_recv()

    def lcopy(src, dst, name):
        return pltpu.make_async_copy(src, dst, lsem.at[LSEM[name]])

    def plane_peer(k):
        z = lax.rem(zc + far_first(lax.div(k, 4)), 4)
        y = lax.rem(yc + far_first(lax.rem(k, 4)), 4)
        return z * 4 + y

    def plane_push(name, src_of, dst_of):
        def body(k, carry):
            p = plane_peer(k)
            rcopy(src_of(k, p), dst_of(k, p), name, (lf, p)).start()
            return carry

        lax.fori_loop(0, BLKS - 1, body, 0)

    local = {}

    def fetch(name, src, dst):
        local[name] = lcopy(src, dst, name)
        local[name].start()

    fetch("rhs", rhs_hbm.at[pl.ds(0, ROWS[0])], rhs0)
    fetch("idx", u_hbm, idx)
    fetch("c01", c_hbm.at[pl.ds(COUP[0, 1], 128)], c01)
    fetch("d0", d_hbm.at[pl.ds(0, 128)], d0)

    barrier = pltpu.get_barrier_semaphore()

    def greet(k, carry):
        pl.semaphore_signal(barrier, inc=1, device_id=(lf, plane_peer(k)), device_id_type=MESH)
        return carry

    lax.fori_loop(0, BLKS - 1, greet, 0)

    def greet_leaf(q, carry):
        pl.semaphore_signal(barrier, inc=1, device_id=(lf ^ q, bk), device_id_type=MESH)
        return carry

    lax.fori_loop(1, 8, greet_leaf, 0)
    local["rhs"].wait()
    ball0[bk] = rhs0[...].T.astype(BF16)
    pl.semaphore_wait(barrier, BLKS - 1 + 7)

    for name, half in (("ag0a", other), ("ag0b", mine)):
        part = ball0.at[bk, pl.ds(half, HALF)]
        plane_push(name, lambda k, p: part, lambda k, p: part)
        sends.append((name, ball0.at[pl.ds(0, BLKS - 1), pl.ds(0, HALF)]))

    def place_of(level, ref, q):
        count = ROWS[level]
        member = (lf ^ q) & ((1 << level) - 1)
        return ref.at[pl.ds(pl.multiple_of(member * count, count), count)]

    def spread(name, level, hbm, start, ref):
        count = ROWS[level]
        src = hbm.at[pl.ds(start, count)]
        for q in range(2, 1 << level, 2):
            rcopy(src, place_of(level, ref, 0), name, (lf ^ q, bk)).start()
        if level == 1:
            rcopy(src, place_of(level, ref, 0), name + "s", sib).start()
            sends.append((name + "s", ref.at[pl.ds(0, count)]))
        else:
            sends.append((name, ref.at[pl.ds(0, BLK // 2 - count)]))
        fetch(name, src, place_of(level, ref, 0))

    def forward(name, level, ref):
        count = ROWS[level]
        local[name].wait()
        arrived(ref.at[pl.ds(0, BLK // 2 - count)], name)
        for q in range(0, 1 << level, 2):
            rcopy(place_of(level, ref, q), place_of(level, ref, q), name + "s", sib).start()
        sends.append((name + "s", ref.at[pl.ds(0, BLK // 2)]))

    def spread_done(name, level, ref):
        if level == 1:
            local[name].wait()
        arrived(ref.at[pl.ds(0, BLK // 2)], name + "s")

    spread("b1", 1, rhs_hbm, STARTS[1], b1)
    spread("d1", 1, d_hbm, STARTS[1], d1)
    fetch("c02", c_hbm.at[pl.ds(COUP[0, 2], 128)], c02)
    fetch("c03", c_hbm.at[pl.ds(COUP[0, 3], 128)], c03)
    spread("c12", 1, c_hbm, COUP[1, 2], c12)
    spread("b2", 2, rhs_hbm, STARTS[2], b2)
    spread("d2", 2, d_hbm, STARTS[2], d2)
    spread("c23", 2, c_hbm, COUP[2, 3], c23)
    spread("c13", 1, c_hbm, COUP[1, 3], c13)

    def expand(c_ref, level, ancestor, store):
        node = lax.div(lf, 1 << level)
        row = PAIR_BASE[level] + node * (3 - level) + (ancestor - level - 1)
        listed = idx[pl.ds(row, 1), :]
        count = ROWS[ancestor]
        bits = count.bit_length() - 1
        place = ((listed >> bits) & (BLKS - 1)) * BLK + (listed >> (bits + 4)) * count + (listed & (count - 1))
        rows = c_ref[...]

        for q in range(W // 256):
            target = lax.broadcasted_iota(jnp.int32, (256, UPD), 0) + q * 256
            hot = jnp.where(target == place, 1.0, 0.0).astype(BF16)
            store(slice(q * 256, (q + 1) * 256), dot_nt(rows, hot).astype(BF16))

    def expand0(ancestor, c_ref):
        a = ancestor - 1

        def store(cols, value):
            x0[a, 0:128, cols] = value

        expand(c_ref, 0, ancestor, store)
        rcopy(x0.at[a, pl.ds(0, 128)], x0.at[a, pl.ds(128, 128)], f"x0{ancestor}", sib).start()
        sends.append((f"x0{ancestor}", x0.at[a, pl.ds(0, 128)]))

    def expand0_done(ancestor):
        arrived(x0.at[ancestor - 1, pl.ds(128, 128)], f"x0{ancestor}")

    def expand_up(level, ancestor, c_ref, x_ref):
        def store(cols, value):
            x_ref[:, cols] = value

        expand(c_ref, level, ancestor, store)

    def permute(level):
        count = ROWS[level]
        lane = lax.broadcasted_iota(jnp.int32, (BLK, BLK), 1)
        for b in range(BLKS):
            total = None
            for m in range(1 << level):
                col = (m * BLKS + b) * count
                tile = draw[level][:, col // BLK * BLK : (col // BLK + 1) * BLK].astype(F32)
                turn = (m * count - col % BLK) % BLK
                if turn:
                    tile = pltpu.roll(tile, turn, 1)
                total = tile if total is None else jnp.where(lane >= m * count, tile, total)
            dperm[level][:, b * BLK : (b + 1) * BLK] = total.astype(BF16)

    def own_rhs(level):
        bt[level - 1] = ball[level][...].T

    def whole(ref, h):
        return jnp.concatenate([ref[h, b] for b in range(BLKS)], axis=1)

    def part(h):
        return pl.ds(pl.multiple_of(mine + h * PART, PART), PART)

    def rows_of(value, h):
        return value[h * PART : (h + 1) * PART]

    def both(values):
        return jnp.concatenate(values, axis=0)

    def scatter(name, h, value, s_ref, r_ref):
        for b in range(BLKS):
            s_ref[h, b] = value[:, b * BLK : (b + 1) * BLK].astype(BF16)
        plane_push(f"{name}{h}", lambda k, p: s_ref.at[h, p], lambda k, p: r_ref.at[h, k])
        sends.append((f"{name}{h}", r_ref.at[h]))

    def scatter_done(name, h, s_ref, r_ref):
        arrived(r_ref.at[h], f"{name}{h}")
        total = s_ref[h, bk].astype(F32)
        for k in range(BLKS - 1):
            total = total + r_ref[h, k].astype(F32)
        return total

    def gather(name, h, value, v_ref):
        v_ref[h, bk] = value.astype(BF16)
        block = v_ref.at[h, bk]
        plane_push(f"{name}{h}", lambda k, p: block, lambda k, p: block)
        sends.append((f"{name}{h}", v_ref.at[h, pl.ds(0, BLKS - 1)]))

    def gather_done(name, h, v_ref):
        arrived(v_ref.at[h, pl.ds(0, BLKS - 1)], f"{name}{h}")
        return whole(v_ref, h)

    def swap(name, h, src, dst, q):
        rcopy(src, dst, f"{name}{h}", (lf ^ q, bk)).start()
        sends.append((f"{name}{h}", dst))

    local["idx"].wait()
    local["c01"].wait()
    expand0(1, c01)

    local["d0"].wait()
    def solve0(name, half):
        arrived(ball0.at[pl.ds(0, BLKS - 1), pl.ds(0, HALF)], name)
        value = dot_nt(jnp.concatenate([ball0[b, pl.ds(half, HALF), :] for b in range(BLKS)], axis=1), d0[...])
        y0r[pl.ds(half, HALF), :] = value
        return value.astype(BF16)

    y0b[...] = solve0("ag0a", other)
    rcopy(y0b, ysib, "y0", sib).start()
    sends.append(("y0", ysib))
    local["c02"].wait()
    expand0(2, c02)
    y0c = solve0("ag0b", mine)
    expand0_done(1)
    arrived(ysib, "y0")
    y0c = jnp.concatenate([y0c, ysib[...]], axis=1)
    for h in (0, 1):
        scatter("rsf1", h, dot_nn(rows_of(y0c, h), x0[0]), sf1, rf1)

    spread_done("b1", 1, b1)
    own_rhs(1)
    spread_done("d1", 1, d1)
    permute(1)
    spread("b3", 3, rhs_hbm, STARTS[3], b3)
    spread("d3", 3, d_hbm, STARTS[3], d3)
    spread_done("c12", 1, c12)
    expand_up(1, 2, c12, x12)
    for h in (0, 1):
        total = scatter_done("rsf1", h, sf1, rf1)
        gather("agf1", h, bt[0, part(h), :] - total, vf1)
    for name, ref in (("b2", b2), ("d2", d2), ("c23", c23)):
        forward(name, 2, ref)
    local["c03"].wait()
    expand0(3, c03)
    expand0_done(2)
    pend = dot_nn(y0c, x0[1])
    y1 = []
    for h in (0, 1):
        y1.append(dot_nt(gather_done("agf1", h, vf1), p1[...]))
        scatter("rsf2", h, rows_of(pend, h) + dot_nn(y1[h].astype(BF16), x12[...]), sf2, rf2)
    y1 = both(y1)

    for name, ref in (("b3", b3), ("d3", d3)):
        forward(name, 3, ref)
    spread_done("b2", 2, b2)
    own_rhs(2)
    spread_done("d2", 2, d2)
    permute(2)
    spread_done("c13", 1, c13)
    expand_up(1, 3, c13, x13)
    for h in (0, 1):
        xs[0, h] = scatter_done("rsf2", h, sf2, rf2).astype(BF16)
        swap("xf2", h, xs.at[0, h], xr2.at[h], 2)
    expand0_done(3)
    pend = dot_nn(y0c, x0[2]) + dot_nn(y1.astype(BF16), x13[...])
    for b in range(BLKS):
        sp3[b] = pend[:, b * BLK : (b + 1) * BLK].astype(BF16)
    plane_push("rsp3", lambda k, p: sp3.at[p], lambda k, p: rp3.at[k])
    sends.append(("rsp3", rp3))
    for h in (0, 1):
        arrived(xr2.at[h], f"xf2{h}")
        gather("agf2", h, bt[1, part(h), :] - (xs[0, h].astype(F32) + xr2[h].astype(F32)), vf2)
    spread_done("c23", 2, c23)
    expand_up(2, 3, c23, x23)
    y2 = []
    for h in (0, 1):
        y2.append(dot_nt(gather_done("agf2", h, vf2), p2[...]))
        scatter("rsf3", h, dot_nn(y2[h].astype(BF16), x23[...]), sf3, rf3)

    arrived(rp3, "rsp3")
    total = sp3[bk].astype(F32)
    for k in range(BLKS - 1):
        total = total + rp3[k].astype(F32)
    total = total.astype(BF16)
    xp[...] = total
    for q in (4, 2, 6):
        rcopy(xp, xp3.at[q // 2 - 1], "xp3", (lf ^ q, bk)).start()
    sends.append(("xp3", xp3))
    spread_done("b3", 3, b3)
    own_rhs(3)
    spread_done("d3", 3, d3)
    permute(3)
    rest = bt[2, pl.ds(mine, HALF), :] - total.astype(F32)
    arrived(xp3, "xp3")
    for q in range(3):
        rest = rest - xp3[q].astype(F32)
    for h in (0, 1):
        xs[1, h] = scatter_done("rsf3", h, sf3, rf3).astype(BF16)
        swap("xf3", h, xs.at[1, h], xr3.at[h], 6)
    for h in (0, 1):
        arrived(xr3.at[h], f"xf3{h}")
        gather("agf3", h, rows_of(rest, h) - (xs[1, h].astype(F32) + xr3[h].astype(F32)), vf3)

    def keep(level, xo_ref):
        rcopy(xo_ref.at[pl.ds(mine, HALF)], xo_ref.at[pl.ds(mine, HALF)], f"xo{level}", sib).start()
        sends.append((f"xo{level}", xo_ref.at[pl.ds(0, HALF)]))

    def write(level, xo_ref):
        arrived(xo_ref.at[pl.ds(0, HALF)], f"xo{level}")
        count = ROWS[level]
        member = lf & ((1 << level) - 1)
        tmp[...] = xo_ref[...].T
        out[pl.ds(STARTS[level], count), :] = tmp[pl.ds(pl.multiple_of(member * count, count), count), :]

    def down(level, xo_ref, s_ref, r_ref, v_ref):
        for h in (0, 1):
            total = scatter_done(f"rsb{level}", h, s_ref, r_ref)
            gather(f"agb{level}", h, total, v_ref)
            xo_ref[part(h), :] = total
        keep(level, xo_ref)

    for h in (0, 1):
        y3 = dot_nt(gather_done("agf3", h, vf3), p3[...])
        scatter("rsb3", h, dot_nn(y3.astype(BF16), p3[...]), sb3, rb3)
    down(3, xo3, sb3, rb3, vb3)

    for h in (0, 1):
        z = y2[h] - dot_nt(gather_done("agb3", h, vb3), x23[...])
        scatter("rsb2", h, dot_nn(z.astype(BF16), p2[...]), sb2, rb2)
    v = both([whole(vb3, 0), whole(vb3, 1)])
    z1 = y1 - dot_nt(v, x13[...])
    t0 = dot_nt(v, x0[2])
    write(3, xo3)
    down(2, xo2, sb2, rb2, vb2)

    for h in (0, 1):
        z = rows_of(z1, h) - dot_nt(gather_done("agb2", h, vb2), x12[...])
        scatter("rsb1", h, dot_nn(z.astype(BF16), p1[...]), sb1, rb1)
    t0 = t0 + dot_nt(both([whole(vb2, 0), whole(vb2, 1)]), x0[1])
    write(2, xo2)
    down(1, xo1, sb1, rb1, vb1)

    def finish0(name, h, start, z):
        value = dot_nn(z.astype(BF16), d0[...])
        place = pl.ds(pl.multiple_of(start + h * PART, PART), PART)
        for b in range(BLKS):
            s0[b, place, :] = value[:, b * BLK : (b + 1) * BLK].astype(BF16)
        plane_push(f"{name}{h}", lambda k, p: s0.at[p, place], lambda k, p: r0.at[k, place])
        sends.append((f"{name}{h}", r0.at[:, pl.ds(0, PART)]))

    for h in (0, 1):
        t = rows_of(t0, h) + dot_nt(gather_done("agb1", h, vb1), x0[0])
        ssend[h] = t[:, BLK:].astype(BF16)
        swap("sx", h, ssend.at[h], srecv.at[h], 1)
        finish0("rs0a", h, mine, y0r[part(h), :] - t[:, :BLK])
    for h in (0, 1):
        arrived(srecv.at[h], f"sx{h}")
        place = pl.ds(pl.multiple_of(other + h * PART, PART), PART)
        finish0("rs0b", h, other, y0r[place, :] - srecv[h].astype(F32))
    write(1, xo1)
    last = ("rs0a0", "rs0a1", "rs0b0", "rs0b1")
    for name, ref in sends:
        if name not in last:
            rcopy(ref, ref, name, sib).wait_send()
    for name in last:
        arrived(r0.at[:, pl.ds(0, PART)], name)
    total = s0[bk].astype(F32)
    for k in range(BLKS - 1):
        total = total + r0[k].astype(F32)
    out[pl.ds(0, 128), :] = total.T
    for name, ref in sends:
        if name in last:
            rcopy(ref, ref, name, sib).wait_send()


def local(right_side, inverse_blocks, coupling, update_rows):
    def vm(*shape, t=BF16):
        return pltpu.VMEM(shape, t)

    block, part = (HALF, BLK), (PART, BLK)
    scratch = (
        [vm(128, CASES, t=F32), vm(34, UPD, t=jnp.int32)]
        + [vm(128, W)] * 7
        + [vm(128, UPD)] * 6
        + [vm(3, 256, W)]
        + [vm(128, W)] * 3
        + [vm(128, CASES, t=F32)] * 3
        + [vm(3, CASES, BLK, t=F32), vm(BLKS, CASES, BLK)]
        + [vm(CASES, BLK, t=F32), vm(*block), vm(*block)]
        + ([vm(2, BLKS, *part)] * 3 + [vm(2, BLKS - 1, *part)] * 3 + [vm(2, BLKS, *part)] * 3) * 2
        + [vm(2, 2, *part), vm(2, *part), vm(2, *part)]
        + [vm(*block), vm(3, *block), vm(BLKS, *block), vm(BLKS - 1, *block)]
        + [vm(2, *part), vm(2, *part)]
        + [vm(BLKS, CASES, BLK), vm(BLKS - 1, CASES, BLK)]
        + [vm(CASES, BLK, t=F32)] * 3
        + [vm(BLK, CASES, t=F32)]
        + [pltpu.SemaphoreType.DMA((len(NAMES),))] * 2
        + [pltpu.SemaphoreType.DMA((len(LOCALS),))]
    )
    result = pl.pallas_call(
        kernel,
        out_shape=jax.ShapeDtypeStruct((240, CASES), F32),
        in_specs=[pl.BlockSpec(memory_space=pltpu.HBM)] * 4,
        out_specs=pl.BlockSpec(memory_space=pltpu.VMEM),
        scratch_shapes=scratch,
        compiler_params=pltpu.CompilerParams(
            collective_id=0, has_side_effects=True, vmem_limit_bytes=56413184
        ),
        name="tree_solve",
    )(right_side[0, 0], inverse_blocks[0, 0], coupling[0, 0], update_rows)
    return result[None, None]


def solution(mesh):
    in_specs = (
        P("leaf", "blk", None, None),
        P("leaf", "blk", None, None),
        P("leaf", "blk", None, None),
        P(),
    )
    out_specs = P("leaf", "blk", None, None)
    return jax.shard_map(local, mesh=mesh, in_specs=in_specs, out_specs=out_specs, check_vma=False)
```

```python
import functools

import jax
import jax.numpy as jnp
from jax import lax
from jax.experimental import pallas as pl
from jax.experimental.pallas import tpu as pltpu
from jax.sharding import PartitionSpec as P

MESH = pl.DeviceIdType.MESH
F32, BF16 = jnp.float32, jnp.bfloat16

W = 2048
UPD = 1024
CASES = 128
HALF = 64
PART = 32
BLKS = 16
BLK = W // BLKS
ROWS = (128, 64, 32, 16)
STARTS = (0, 128, 192, 224)
COUP = {(0, 1): 0, (0, 2): 128, (0, 3): 256, (1, 2): 384, (1, 3): 448, (2, 3): 512}
PAIR_BASE = (0, 24, 32)

NAMES = (
    ["ag0a", "ag0b", "x01", "x02", "x03", "y0"]
    + [f"{name}{way}" for name in ("d1", "c12", "c13", "b1", "d2", "c23", "b2", "d3", "b3") for way in ("", "s")]
    + [f"{name}{l}{h}" for name in ("rsf", "agf", "rsb", "agb") for l in (1, 2, 3) for h in (0, 1)]
    + [f"{name}{h}" for name in ("xf2", "xf3", "sx", "rs0a", "rs0b") for h in (0, 1)]
    + ["rsp3", "xp3", "xo1", "xo2", "xo3"]
)
SEM = {name: i for i, name in enumerate(NAMES)}
LOCALS = ["rhs", "d0", "idx", "c01", "c02", "c03", "d1", "d2", "d3", "c12", "c13", "c23", "b1", "b2", "b3"]
LSEM = {name: i for i, name in enumerate(LOCALS)}


def dot_nt(a, b):
    return lax.dot_general(a, b, (((1,), (1,)), ((), ())), preferred_element_type=F32)


def dot_nn(a, b):
    return jnp.dot(a, b, preferred_element_type=F32)


def far_first(i):
    return jnp.where(i < 2, 2 - i, jnp.where(i == 2, 3, 0))


def kernel(
    rhs_hbm, d_hbm, c_hbm, u_hbm, out,
    rhs0, idx, d0, d1, d2, d3, p1, p2, p3, c01, c02, c03, c12, c13, c23,
    x0, x12, x13, x23, b1, b2, b3, bt, ball0, y0r, y0b, ysib,
    sf1, sf2, sf3, rf1, rf2, rf3, vf1, vf2, vf3,
    sb1, sb2, sb3, rb1, rb2, rb3, vb1, vb2, vb3,
    xs, xr2, xr3, xp, xp3, sp3, rp3, ssend, srecv, s0, r0, xo1, xo2, xo3, tmp,
    ssem, rsem, lsem,
):
    lf, bk = lax.axis_index("leaf"), lax.axis_index("blk")
    core = lax.rem(lf, 2)
    mine = pl.multiple_of(core * HALF, HALF)
    other = pl.multiple_of((1 - core) * HALF, HALF)
    zc, yc = lax.div(bk, 4), lax.rem(bk, 4)
    sib = (lf ^ 1, bk)
    draw, dperm = (d0, d1, d2, d3), (None, p1, p2, p3)
    ball = (None, b1, b2, b3)
    sends = []

    def rcopy(src, dst, name, dev):
        i = SEM[name]
        return pltpu.make_async_remote_copy(
            src_ref=src, dst_ref=dst, send_sem=ssem.at[i], recv_sem=rsem.at[i], device_id=dev, device_id_type=MESH
        )

    def arrived(ref, name):
        rcopy(ref, ref, name, sib).wait_recv()

    def lcopy(src, dst, name):
        return pltpu.make_async_copy(src, dst, lsem.at[LSEM[name]])

    def plane_peer(k):
        z = lax.rem(zc + far_first(lax.div(k, 4)), 4)
        y = lax.rem(yc + far_first(lax.rem(k, 4)), 4)
        return z * 4 + y

    def plane_push(name, src_of, dst_of):
        def body(k, carry):
            p = plane_peer(k)
            rcopy(src_of(k, p), dst_of(k, p), name, (lf, p)).start()
            return carry

        lax.fori_loop(0, BLKS - 1, body, 0)

    local = {}

    def fetch(name, src, dst):
        local[name] = lcopy(src, dst, name)
        local[name].start()

    fetch("rhs", rhs_hbm.at[pl.ds(0, ROWS[0])], rhs0)
    fetch("idx", u_hbm, idx)
    fetch("c01", c_hbm.at[pl.ds(COUP[0, 1], 128)], c01)
    fetch("d0", d_hbm.at[pl.ds(0, 128)], d0)

    barrier = pltpu.get_barrier_semaphore()

    def greet(k, carry):
        pl.semaphore_signal(barrier, inc=1, device_id=(lf, plane_peer(k)), device_id_type=MESH)
        return carry

    lax.fori_loop(0, BLKS - 1, greet, 0)

    def greet_leaf(q, carry):
        pl.semaphore_signal(barrier, inc=1, device_id=(lf ^ q, bk), device_id_type=MESH)
        return carry

    lax.fori_loop(1, 8, greet_leaf, 0)
    local["rhs"].wait()
    ball0[bk] = rhs0[...].T.astype(BF16)
    pl.semaphore_wait(barrier, BLKS - 1 + 7)

    for name, half in (("ag0a", other), ("ag0b", mine)):
        part = ball0.at[bk, pl.ds(half, HALF)]
        plane_push(name, lambda k, p: part, lambda k, p: part)
        sends.append((name, ball0.at[pl.ds(0, BLKS - 1), pl.ds(0, HALF)]))

    def place_of(level, ref, q):
        count = ROWS[level]
        member = (lf ^ q) & ((1 << level) - 1)
        return ref.at[pl.ds(pl.multiple_of(member * count, count), count)]

    def spread(name, level, hbm, start, ref):
        count = ROWS[level]
        src = hbm.at[pl.ds(start, count)]
        for q in range(2, 1 << level, 2):
            rcopy(src, place_of(level, ref, 0), name, (lf ^ q, bk)).start()
        if level == 1:
            rcopy(src, place_of(level, ref, 0), name + "s", sib).start()
            sends.append((name + "s", ref.at[pl.ds(0, count)]))
        else:
            sends.append((name, ref.at[pl.ds(0, BLK // 2 - count)]))
        fetch(name, src, place_of(level, ref, 0))

    def forward(name, level, ref):
        count = ROWS[level]
        local[name].wait()
        arrived(ref.at[pl.ds(0, BLK // 2 - count)], name)
        for q in range(0, 1 << level, 2):
            rcopy(place_of(level, ref, q), place_of(level, ref, q), name + "s", sib).start()
        sends.append((name + "s", ref.at[pl.ds(0, BLK // 2)]))

    def spread_done(name, level, ref):
        if level == 1:
            local[name].wait()
        arrived(ref.at[pl.ds(0, BLK // 2)], name + "s")

    spread("b1", 1, rhs_hbm, STARTS[1], b1)
    spread("d1", 1, d_hbm, STARTS[1], d1)
    fetch("c02", c_hbm.at[pl.ds(COUP[0, 2], 128)], c02)
    fetch("c03", c_hbm.at[pl.ds(COUP[0, 3], 128)], c03)
    spread("c12", 1, c_hbm, COUP[1, 2], c12)
    spread("b2", 2, rhs_hbm, STARTS[2], b2)
    spread("d2", 2, d_hbm, STARTS[2], d2)
    spread("c23", 2, c_hbm, COUP[2, 3], c23)
    spread("c13", 1, c_hbm, COUP[1, 3], c13)

    def expand(c_ref, level, ancestor, store):
        node = lax.div(lf, 1 << level)
        row = PAIR_BASE[level] + node * (3 - level) + (ancestor - level - 1)
        listed = idx[pl.ds(row, 1), :]
        count = ROWS[ancestor]
        bits = count.bit_length() - 1
        place = ((listed >> bits) & (BLKS - 1)) * BLK + (listed >> (bits + 4)) * count + (listed & (count - 1))
        rows = c_ref[...]

        for q in range(W // 256):
            target = lax.broadcasted_iota(jnp.int32, (256, UPD), 0) + q * 256
            hot = jnp.where(target == place, 1.0, 0.0).astype(BF16)
            store(slice(q * 256, (q + 1) * 256), dot_nt(rows, hot).astype(BF16))

    def expand0(ancestor, c_ref):
        a = ancestor - 1

        def store(cols, value):
            x0[a, 0:128, cols] = value

        expand(c_ref, 0, ancestor, store)
        rcopy(x0.at[a, pl.ds(0, 128)], x0.at[a, pl.ds(128, 128)], f"x0{ancestor}", sib).start()
        sends.append((f"x0{ancestor}", x0.at[a, pl.ds(0, 128)]))

    def expand0_done(ancestor):
        arrived(x0.at[ancestor - 1, pl.ds(128, 128)], f"x0{ancestor}")

    def expand_up(level, ancestor, c_ref, x_ref):
        def store(cols, value):
            x_ref[:, cols] = value

        expand(c_ref, level, ancestor, store)

    def permute(level):
        count = ROWS[level]
        lane = lax.broadcasted_iota(jnp.int32, (BLK, BLK), 1)
        for b in range(BLKS):
            total = None
            for m in range(1 << level):
                col = (m * BLKS + b) * count
                tile = draw[level][:, col // BLK * BLK : (col // BLK + 1) * BLK].astype(F32)
                turn = (m * count - col % BLK) % BLK
                if turn:
                    tile = pltpu.roll(tile, turn, 1)
                total = tile if total is None else jnp.where(lane >= m * count, tile, total)
            dperm[level][:, b * BLK : (b + 1) * BLK] = total.astype(BF16)

    def own_rhs(level):
        bt[level - 1] = ball[level][...].T

    def whole(ref, h):
        return jnp.concatenate([ref[h, b] for b in range(BLKS)], axis=1)

    def part(h):
        return pl.ds(pl.multiple_of(mine + h * PART, PART), PART)

    def rows_of(value, h):
        return value[h * PART : (h + 1) * PART]

    def both(values):
        return jnp.concatenate(values, axis=0)

    def scatter(name, h, value, s_ref, r_ref):
        for b in range(BLKS):
            s_ref[h, b] = value[:, b * BLK : (b + 1) * BLK].astype(BF16)
        plane_push(f"{name}{h}", lambda k, p: s_ref.at[h, p], lambda k, p: r_ref.at[h, k])
        sends.append((f"{name}{h}", r_ref.at[h]))

    def scatter_done(name, h, s_ref, r_ref):
        arrived(r_ref.at[h], f"{name}{h}")
        total = s_ref[h, bk].astype(F32)
        for k in range(BLKS - 1):
            total = total + r_ref[h, k].astype(F32)
        return total

    def gather(name, h, value, v_ref):
        v_ref[h, bk] = value.astype(BF16)
        block = v_ref.at[h, bk]
        plane_push(f"{name}{h}", lambda k, p: block, lambda k, p: block)
        sends.append((f"{name}{h}", v_ref.at[h, pl.ds(0, BLKS - 1)]))

    def gather_done(name, h, v_ref):
        arrived(v_ref.at[h, pl.ds(0, BLKS - 1)], f"{name}{h}")
        return whole(v_ref, h)

    def swap(name, h, src, dst, q):
        rcopy(src, dst, f"{name}{h}", (lf ^ q, bk)).start()
        sends.append((f"{name}{h}", dst))

    local["idx"].wait()
    local["c01"].wait()
    expand0(1, c01)

    local["d0"].wait()
    def solve0(name, half):
        arrived(ball0.at[pl.ds(0, BLKS - 1), pl.ds(0, HALF)], name)
        value = dot_nt(jnp.concatenate([ball0[b, pl.ds(half, HALF), :] for b in range(BLKS)], axis=1), d0[...])
        y0r[pl.ds(half, HALF), :] = value
        return value.astype(BF16)

    y0b[...] = solve0("ag0a", other)
    rcopy(y0b, ysib, "y0", sib).start()
    sends.append(("y0", ysib))
    local["c02"].wait()
    expand0(2, c02)
    y0c = solve0("ag0b", mine)
    expand0_done(1)
    arrived(ysib, "y0")
    y0c = jnp.concatenate([y0c, ysib[...]], axis=1)
    for h in (0, 1):
        scatter("rsf1", h, dot_nn(rows_of(y0c, h), x0[0]), sf1, rf1)

    spread_done("b1", 1, b1)
    own_rhs(1)
    spread_done("d1", 1, d1)
    permute(1)
    spread("b3", 3, rhs_hbm, STARTS[3], b3)
    spread("d3", 3, d_hbm, STARTS[3], d3)
    spread_done("c12", 1, c12)
    expand_up(1, 2, c12, x12)
    for h in (0, 1):
        total = scatter_done("rsf1", h, sf1, rf1)
        gather("agf1", h, bt[0, part(h), :] - total, vf1)
    for name, ref in (("b2", b2), ("d2", d2), ("c23", c23)):
        forward(name, 2, ref)
    local["c03"].wait()
    expand0(3, c03)
    expand0_done(2)
    pend = dot_nn(y0c, x0[1])
    y1 = []
    for h in (0, 1):
        y1.append(dot_nt(gather_done("agf1", h, vf1), p1[...]))
        scatter("rsf2", h, rows_of(pend, h) + dot_nn(y1[h].astype(BF16), x12[...]), sf2, rf2)
    y1 = both(y1)

    for name, ref in (("b3", b3), ("d3", d3)):
        forward(name, 3, ref)
    spread_done("b2", 2, b2)
    own_rhs(2)
    spread_done("d2", 2, d2)
    permute(2)
    spread_done("c13", 1, c13)
    expand_up(1, 3, c13, x13)
    for h in (0, 1):
        xs[0, h] = scatter_done("rsf2", h, sf2, rf2).astype(BF16)
        swap("xf2", h, xs.at[0, h], xr2.at[h], 2)
    expand0_done(3)
    pend = dot_nn(y0c, x0[2]) + dot_nn(y1.astype(BF16), x13[...])
    for b in range(BLKS):
        sp3[b] = pend[:, b * BLK : (b + 1) * BLK].astype(BF16)
    plane_push("rsp3", lambda k, p: sp3.at[p], lambda k, p: rp3.at[k])
    sends.append(("rsp3", rp3))
    for h in (0, 1):
        arrived(xr2.at[h], f"xf2{h}")
        gather("agf2", h, bt[1, part(h), :] - (xs[0, h].astype(F32) + xr2[h].astype(F32)), vf2)
    spread_done("c23", 2, c23)
    expand_up(2, 3, c23, x23)
    y2 = []
    for h in (0, 1):
        y2.append(dot_nt(gather_done("agf2", h, vf2), p2[...]))
        scatter("rsf3", h, dot_nn(y2[h].astype(BF16), x23[...]), sf3, rf3)

    arrived(rp3, "rsp3")
    total = sp3[bk].astype(F32)
    for k in range(BLKS - 1):
        total = total + rp3[k].astype(F32)
    total = total.astype(BF16)
    xp[...] = total
    for q in (4, 2, 6):
        rcopy(xp, xp3.at[q // 2 - 1], "xp3", (lf ^ q, bk)).start()
    sends.append(("xp3", xp3))
    spread_done("b3", 3, b3)
    own_rhs(3)
    spread_done("d3", 3, d3)
    permute(3)
    rest = bt[2, pl.ds(mine, HALF), :] - total.astype(F32)
    arrived(xp3, "xp3")
    for q in range(3):
        rest = rest - xp3[q].astype(F32)
    for h in (0, 1):
        xs[1, h] = scatter_done("rsf3", h, sf3, rf3).astype(BF16)
        swap("xf3", h, xs.at[1, h], xr3.at[h], 6)
    for h in (0, 1):
        arrived(xr3.at[h], f"xf3{h}")
        gather("agf3", h, rows_of(rest, h) - (xs[1, h].astype(F32) + xr3[h].astype(F32)), vf3)

    def keep(level, xo_ref):
        rcopy(xo_ref.at[pl.ds(mine, HALF)], xo_ref.at[pl.ds(mine, HALF)], f"xo{level}", sib).start()
        sends.append((f"xo{level}", xo_ref.at[pl.ds(0, HALF)]))

    def write(level, xo_ref):
        arrived(xo_ref.at[pl.ds(0, HALF)], f"xo{level}")
        count = ROWS[level]
        member = lf & ((1 << level) - 1)
        tmp[...] = xo_ref[...].T
        out[pl.ds(STARTS[level], count), :] = tmp[pl.ds(pl.multiple_of(member * count, count), count), :]

    def down(level, xo_ref, s_ref, r_ref, v_ref):
        for h in (0, 1):
            total = scatter_done(f"rsb{level}", h, s_ref, r_ref)
            gather(f"agb{level}", h, total, v_ref)
            xo_ref[part(h), :] = total
        keep(level, xo_ref)

    for h in (0, 1):
        y3 = dot_nt(gather_done("agf3", h, vf3), p3[...])
        scatter("rsb3", h, dot_nn(y3.astype(BF16), p3[...]), sb3, rb3)
    down(3, xo3, sb3, rb3, vb3)

    for h in (0, 1):
        z = y2[h] - dot_nt(gather_done("agb3", h, vb3), x23[...])
        scatter("rsb2", h, dot_nn(z.astype(BF16), p2[...]), sb2, rb2)
    v = both([whole(vb3, 0), whole(vb3, 1)])
    z1 = y1 - dot_nt(v, x13[...])
    t0 = dot_nt(v, x0[2])
    write(3, xo3)
    down(2, xo2, sb2, rb2, vb2)

    for h in (0, 1):
        z = rows_of(z1, h) - dot_nt(gather_done("agb2", h, vb2), x12[...])
        scatter("rsb1", h, dot_nn(z.astype(BF16), p1[...]), sb1, rb1)
    t0 = t0 + dot_nt(both([whole(vb2, 0), whole(vb2, 1)]), x0[1])
    write(2, xo2)
    down(1, xo1, sb1, rb1, vb1)

    def finish0(name, h, start, z):
        value = dot_nn(z.astype(BF16), d0[...])
        place = pl.ds(pl.multiple_of(start + h * PART, PART), PART)
        for b in range(BLKS):
            s0[b, place, :] = value[:, b * BLK : (b + 1) * BLK].astype(BF16)
        plane_push(f"{name}{h}", lambda k, p: s0.at[p, place], lambda k, p: r0.at[k, place])
        sends.append((f"{name}{h}", r0.at[:, pl.ds(0, PART)]))

    for h in (0, 1):
        v = gather_done("agb1", h, vb1)
        before = rows_of(t0, h)
        ssend[h] = (before[:, BLK:] + dot_nt(v, x0[0, BLK:])).astype(BF16)
        swap("sx", h, ssend.at[h], srecv.at[h], 1)
        finish0("rs0a", h, mine, y0r[part(h), :] - (before[:, :BLK] + dot_nt(v, x0[0, :BLK])))
    for h in (0, 1):
        arrived(srecv.at[h], f"sx{h}")
        place = pl.ds(pl.multiple_of(other + h * PART, PART), PART)
        finish0("rs0b", h, other, y0r[place, :] - srecv[h].astype(F32))
    write(1, xo1)
    last = ("rs0a0", "rs0a1", "rs0b0", "rs0b1")
    for name, ref in sends:
        if name not in last:
            rcopy(ref, ref, name, sib).wait_send()
    for name in last:
        arrived(r0.at[:, pl.ds(0, PART)], name)
    total = s0[bk].astype(F32)
    for k in range(BLKS - 1):
        total = total + r0[k].astype(F32)
    out[pl.ds(0, 128), :] = total.T
    for name, ref in sends:
        if name in last:
            rcopy(ref, ref, name, sib).wait_send()


def local(right_side, inverse_blocks, coupling, update_rows):
    def vm(*shape, t=BF16):
        return pltpu.VMEM(shape, t)

    block, part = (HALF, BLK), (PART, BLK)
    scratch = (
        [vm(128, CASES, t=F32), vm(34, UPD, t=jnp.int32)]
        + [vm(128, W)] * 7
        + [vm(128, UPD)] * 6
        + [vm(3, 256, W)]
        + [vm(128, W)] * 3
        + [vm(128, CASES, t=F32)] * 3
        + [vm(3, CASES, BLK, t=F32), vm(BLKS, CASES, BLK)]
        + [vm(CASES, BLK, t=F32), vm(*block), vm(*block)]
        + ([vm(2, BLKS, *part)] * 3 + [vm(2, BLKS - 1, *part)] * 3 + [vm(2, BLKS, *part)] * 3) * 2
        + [vm(2, 2, *part), vm(2, *part), vm(2, *part)]
        + [vm(*block), vm(3, *block), vm(BLKS, *block), vm(BLKS - 1, *block)]
        + [vm(2, *part), vm(2, *part)]
        + [vm(BLKS, CASES, BLK), vm(BLKS - 1, CASES, BLK)]
        + [vm(CASES, BLK, t=F32)] * 3
        + [vm(BLK, CASES, t=F32)]
        + [pltpu.SemaphoreType.DMA((len(NAMES),))] * 2
        + [pltpu.SemaphoreType.DMA((len(LOCALS),))]
    )
    result = pl.pallas_call(
        kernel,
        out_shape=jax.ShapeDtypeStruct((240, CASES), F32),
        in_specs=[pl.BlockSpec(memory_space=pltpu.HBM)] * 4,
        out_specs=pl.BlockSpec(memory_space=pltpu.VMEM),
        scratch_shapes=scratch,
        compiler_params=pltpu.CompilerParams(
            collective_id=0, has_side_effects=True, vmem_limit_bytes=56413184
        ),
        name="tree_solve",
    )(right_side[0, 0], inverse_blocks[0, 0], coupling[0, 0], update_rows)
    return result[None, None]


def solution(mesh):
    in_specs = (
        P("leaf", "blk", None, None),
        P("leaf", "blk", None, None),
        P("leaf", "blk", None, None),
        P(),
    )
    out_specs = P("leaf", "blk", None, None)
    return jax.shard_map(local, mesh=mesh, in_specs=in_specs, out_specs=out_specs, check_vma=False)
```

```python
import functools

import jax
import jax.numpy as jnp
from jax import lax
from jax.experimental import pallas as pl
from jax.experimental.pallas import tpu as pltpu
from jax.sharding import PartitionSpec as P

MESH = pl.DeviceIdType.MESH
F32, BF16 = jnp.float32, jnp.bfloat16

W = 2048
UPD = 1024
CASES = 128
HALF = 64
PART = 32
BLKS = 16
BLK = W // BLKS
ROWS = (128, 64, 32, 16)
STARTS = (0, 128, 192, 224)
COUP = {(0, 1): 0, (0, 2): 128, (0, 3): 256, (1, 2): 384, (1, 3): 448, (2, 3): 512}
PAIR_BASE = (0, 24, 32)

NAMES = (
    ["ag0a", "ag0b", "x01", "x02", "x03", "y0"]
    + [f"{name}{way}" for name in ("d1", "c12", "c13", "b1", "d2", "c23", "b2", "d3", "b3") for way in ("", "s")]
    + [f"{name}{l}{h}" for name in ("rsf", "agf", "rsb", "agb") for l in (1, 2, 3) for h in (0, 1)]
    + [f"{name}{h}" for name in ("xf2", "xf3", "sx", "rs0a", "rs0b") for h in (0, 1)]
    + ["rsp3", "xp3", "xo1", "xo2", "xo3"]
)
SEM = {name: i for i, name in enumerate(NAMES)}
LOCALS = ["rhs", "d0", "idx", "c01", "c02", "c03", "d1", "d2", "d3", "c12", "c13", "c23", "b1", "b2", "b3"]
LSEM = {name: i for i, name in enumerate(LOCALS)}


def dot_nt(a, b):
    return lax.dot_general(a, b, (((1,), (1,)), ((), ())), preferred_element_type=F32)


def dot_nn(a, b):
    return jnp.dot(a, b, preferred_element_type=F32)


def far_first(i):
    return jnp.where(i < 2, 2 - i, jnp.where(i == 2, 3, 0))


def kernel(
    rhs_hbm, d_hbm, c_hbm, u_hbm, out,
    rhs0, idx, d0, d1, d2, d3, p1, p2, p3, c01, c02, c03, c12, c13, c23,
    x0, x12, x13, x23, b1, b2, b3, bt, ball0, y0r, y0b, ysib,
    sf1, sf2, sf3, rf1, rf2, rf3, vf1, vf2, vf3,
    sb1, sb2, sb3, rb1, rb2, rb3, vb1, vb2, vb3,
    xs, xr2, xr3, xp, xp3, sp3, rp3, ssend, srecv, s0, r0, xo1, xo2, xo3, tmp,
    ssem, rsem, lsem,
):
    lf, bk = lax.axis_index("leaf"), lax.axis_index("blk")
    core = lax.rem(lf, 2)
    mine = pl.multiple_of(core * HALF, HALF)
    other = pl.multiple_of((1 - core) * HALF, HALF)
    zc, yc = lax.div(bk, 4), lax.rem(bk, 4)
    sib = (lf ^ 1, bk)
    draw, dperm = (d0, d1, d2, d3), (None, p1, p2, p3)
    ball = (None, b1, b2, b3)
    sends = []

    def rcopy(src, dst, name, dev):
        i = SEM[name]
        return pltpu.make_async_remote_copy(
            src_ref=src, dst_ref=dst, send_sem=ssem.at[i], recv_sem=rsem.at[i], device_id=dev, device_id_type=MESH
        )

    def arrived(ref, name):
        rcopy(ref, ref, name, sib).wait_recv()

    def lcopy(src, dst, name):
        return pltpu.make_async_copy(src, dst, lsem.at[LSEM[name]])

    def plane_peer(k):
        z = lax.rem(zc + far_first(lax.div(k, 4)), 4)
        y = lax.rem(yc + far_first(lax.rem(k, 4)), 4)
        return z * 4 + y

    def plane_push(name, src_of, dst_of):
        def body(k, carry):
            p = plane_peer(k)
            rcopy(src_of(k, p), dst_of(k, p), name, (lf, p)).start()
            return carry

        lax.fori_loop(0, BLKS - 1, body, 0)

    local = {}

    def fetch(name, src, dst):
        local[name] = lcopy(src, dst, name)
        local[name].start()

    fetch("rhs", rhs_hbm.at[pl.ds(0, ROWS[0])], rhs0)
    fetch("idx", u_hbm, idx)
    fetch("c01", c_hbm.at[pl.ds(COUP[0, 1], 128)], c01)
    fetch("d0", d_hbm.at[pl.ds(0, 128)], d0)

    barrier = pltpu.get_barrier_semaphore()

    def greet(k, carry):
        pl.semaphore_signal(barrier, inc=1, device_id=(lf, plane_peer(k)), device_id_type=MESH)
        return carry

    lax.fori_loop(0, BLKS - 1, greet, 0)

    def greet_leaf(q, carry):
        pl.semaphore_signal(barrier, inc=1, device_id=(lf ^ q, bk), device_id_type=MESH)
        return carry

    lax.fori_loop(1, 8, greet_leaf, 0)
    local["rhs"].wait()
    ball0[bk] = rhs0[...].T.astype(BF16)
    pl.semaphore_wait(barrier, BLKS - 1 + 7)

    for name, half in (("ag0a", other), ("ag0b", mine)):
        part = ball0.at[bk, pl.ds(half, HALF)]
        plane_push(name, lambda k, p: part, lambda k, p: part)
        sends.append((name, ball0.at[pl.ds(0, BLKS - 1), pl.ds(0, HALF)]))

    def place_of(level, ref, q):
        count = ROWS[level]
        member = (lf ^ q) & ((1 << level) - 1)
        return ref.at[pl.ds(pl.multiple_of(member * count, count), count)]

    def spread(name, level, hbm, start, ref):
        count = ROWS[level]
        src = hbm.at[pl.ds(start, count)]
        for q in range(2, 1 << level, 2):
            rcopy(src, place_of(level, ref, 0), name, (lf ^ q, bk)).start()
        if level == 1:
            rcopy(src, place_of(level, ref, 0), name + "s", sib).start()
            sends.append((name + "s", ref.at[pl.ds(0, count)]))
        else:
            sends.append((name, ref.at[pl.ds(0, BLK // 2 - count)]))
        fetch(name, src, place_of(level, ref, 0))

    def forward(name, level, ref):
        count = ROWS[level]
        local[name].wait()
        arrived(ref.at[pl.ds(0, BLK // 2 - count)], name)
        for q in range(0, 1 << level, 2):
            rcopy(place_of(level, ref, q), place_of(level, ref, q), name + "s", sib).start()
        sends.append((name + "s", ref.at[pl.ds(0, BLK // 2)]))

    def spread_done(name, level, ref):
        if level == 1:
            local[name].wait()
        arrived(ref.at[pl.ds(0, BLK // 2)], name + "s")

    spread("b1", 1, rhs_hbm, STARTS[1], b1)
    spread("d1", 1, d_hbm, STARTS[1], d1)
    fetch("c02", c_hbm.at[pl.ds(COUP[0, 2], 128)], c02)
    fetch("c03", c_hbm.at[pl.ds(COUP[0, 3], 128)], c03)
    spread("c12", 1, c_hbm, COUP[1, 2], c12)
    spread("b2", 2, rhs_hbm, STARTS[2], b2)
    spread("d2", 2, d_hbm, STARTS[2], d2)
    spread("c23", 2, c_hbm, COUP[2, 3], c23)
    spread("c13", 1, c_hbm, COUP[1, 3], c13)

    def expand(c_ref, level, ancestor, store):
        node = lax.div(lf, 1 << level)
        row = PAIR_BASE[level] + node * (3 - level) + (ancestor - level - 1)
        listed = idx[pl.ds(row, 1), :]
        count = ROWS[ancestor]
        bits = count.bit_length() - 1
        place = ((listed >> bits) & (BLKS - 1)) * BLK + (listed >> (bits + 4)) * count + (listed & (count - 1))
        rows = c_ref[...]

        for q in range(W // 256):
            target = lax.broadcasted_iota(jnp.int32, (256, UPD), 0) + q * 256
            hot = jnp.where(target == place, 1.0, 0.0).astype(BF16)
            store(slice(q * 256, (q + 1) * 256), dot_nt(rows, hot).astype(BF16))

    def expand0(ancestor, c_ref):
        a = ancestor - 1

        def store(cols, value):
            x0[a, 0:128, cols] = value

        expand(c_ref, 0, ancestor, store)
        rcopy(x0.at[a, pl.ds(0, 128)], x0.at[a, pl.ds(128, 128)], f"x0{ancestor}", sib).start()
        sends.append((f"x0{ancestor}", x0.at[a, pl.ds(0, 128)]))

    def expand0_done(ancestor):
        arrived(x0.at[ancestor - 1, pl.ds(128, 128)], f"x0{ancestor}")

    def expand_up(level, ancestor, c_ref, x_ref):
        def store(cols, value):
            x_ref[:, cols] = value

        expand(c_ref, level, ancestor, store)

    def permute(level):
        count = ROWS[level]
        lane = lax.broadcasted_iota(jnp.int32, (BLK, BLK), 1)
        for b in range(BLKS):
            total = None
            for m in range(1 << level):
                col = (m * BLKS + b) * count
                tile = draw[level][:, col // BLK * BLK : (col // BLK + 1) * BLK].astype(F32)
                turn = (m * count - col % BLK) % BLK
                if turn:
                    tile = pltpu.roll(tile, turn, 1)
                total = tile if total is None else jnp.where(lane >= m * count, tile, total)
            dperm[level][:, b * BLK : (b + 1) * BLK] = total.astype(BF16)

    def own_rhs(level):
        bt[level - 1] = ball[level][...].T

    def whole(ref, h):
        return jnp.concatenate([ref[h, b] for b in range(BLKS)], axis=1)

    def part(h):
        return pl.ds(pl.multiple_of(mine + h * PART, PART), PART)

    def rows_of(value, h):
        return value[h * PART : (h + 1) * PART]

    def both(values):
        return jnp.concatenate(values, axis=0)

    def scatter(name, h, value, s_ref, r_ref):
        for b in range(BLKS):
            s_ref[h, b] = value[:, b * BLK : (b + 1) * BLK].astype(BF16)
        plane_push(f"{name}{h}", lambda k, p: s_ref.at[h, p], lambda k, p: r_ref.at[h, k])
        sends.append((f"{name}{h}", r_ref.at[h]))

    def scatter_done(name, h, s_ref, r_ref):
        arrived(r_ref.at[h], f"{name}{h}")
        total = s_ref[h, bk].astype(F32)
        for k in range(BLKS - 1):
            total = total + r_ref[h, k].astype(F32)
        return total

    def gather(name, h, value, v_ref):
        v_ref[h, bk] = value.astype(BF16)
        block = v_ref.at[h, bk]
        plane_push(f"{name}{h}", lambda k, p: block, lambda k, p: block)
        sends.append((f"{name}{h}", v_ref.at[h, pl.ds(0, BLKS - 1)]))

    def gather_done(name, h, v_ref):
        arrived(v_ref.at[h, pl.ds(0, BLKS - 1)], f"{name}{h}")
        return whole(v_ref, h)

    def swap(name, h, src, dst, q):
        rcopy(src, dst, f"{name}{h}", (lf ^ q, bk)).start()
        sends.append((f"{name}{h}", dst))

    local["idx"].wait()
    local["c01"].wait()
    expand0(1, c01)

    local["d0"].wait()
    def solve0(name, half):
        arrived(ball0.at[pl.ds(0, BLKS - 1), pl.ds(0, HALF)], name)
        value = dot_nt(jnp.concatenate([ball0[b, pl.ds(half, HALF), :] for b in range(BLKS)], axis=1), d0[...])
        y0r[pl.ds(half, HALF), :] = value
        return value.astype(BF16)

    y0b[...] = solve0("ag0a", other)
    rcopy(y0b, ysib, "y0", sib).start()
    sends.append(("y0", ysib))
    local["c02"].wait()
    expand0(2, c02)
    y0c = solve0("ag0b", mine)
    expand0_done(1)
    arrived(ysib, "y0")
    y0c = jnp.concatenate([y0c, ysib[...]], axis=1)
    for h in (0, 1):
        scatter("rsf1", h, dot_nn(rows_of(y0c, h), x0[0]), sf1, rf1)

    spread_done("b1", 1, b1)
    own_rhs(1)
    spread_done("d1", 1, d1)
    permute(1)
    spread("b3", 3, rhs_hbm, STARTS[3], b3)
    spread("d3", 3, d_hbm, STARTS[3], d3)
    spread_done("c12", 1, c12)
    expand_up(1, 2, c12, x12)
    for h in (0, 1):
        total = scatter_done("rsf1", h, sf1, rf1)
        gather("agf1", h, bt[0, part(h), :] - total, vf1)
    for name, ref in (("b2", b2), ("d2", d2), ("c23", c23)):
        forward(name, 2, ref)
    local["c03"].wait()
    expand0(3, c03)
    expand0_done(2)
    pend = dot_nn(y0c, x0[1])
    y1 = []
    for h in (0, 1):
        y1.append(dot_nt(gather_done("agf1", h, vf1), p1[...]))
        scatter("rsf2", h, rows_of(pend, h) + dot_nn(y1[h].astype(BF16), x12[...]), sf2, rf2)
    y1 = both(y1)

    for name, ref in (("b3", b3), ("d3", d3)):
        forward(name, 3, ref)
    spread_done("b2", 2, b2)
    own_rhs(2)
    spread_done("d2", 2, d2)
    permute(2)
    spread_done("c13", 1, c13)
    expand_up(1, 3, c13, x13)
    for h in (0, 1):
        xs[0, h] = scatter_done("rsf2", h, sf2, rf2).astype(BF16)
        swap("xf2", h, xs.at[0, h], xr2.at[h], 2)
    expand0_done(3)
    pend = dot_nn(y0c, x0[2]) + dot_nn(y1.astype(BF16), x13[...])
    for b in range(BLKS):
        sp3[b] = pend[:, b * BLK : (b + 1) * BLK].astype(BF16)
    plane_push("rsp3", lambda k, p: sp3.at[p], lambda k, p: rp3.at[k])
    sends.append(("rsp3", rp3))
    for h in (0, 1):
        arrived(xr2.at[h], f"xf2{h}")
        gather("agf2", h, bt[1, part(h), :] - (xs[0, h].astype(F32) + xr2[h].astype(F32)), vf2)
    spread_done("c23", 2, c23)
    expand_up(2, 3, c23, x23)
    y2 = []
    for h in (0, 1):
        y2.append(dot_nt(gather_done("agf2", h, vf2), p2[...]))
        scatter("rsf3", h, dot_nn(y2[h].astype(BF16), x23[...]), sf3, rf3)

    arrived(rp3, "rsp3")
    total = sp3[bk].astype(F32)
    for k in range(BLKS - 1):
        total = total + rp3[k].astype(F32)
    total = total.astype(BF16)
    xp[...] = total
    for q in (4, 2, 6):
        rcopy(xp, xp3.at[q // 2 - 1], "xp3", (lf ^ q, bk)).start()
    sends.append(("xp3", xp3))
    spread_done("b3", 3, b3)
    own_rhs(3)
    spread_done("d3", 3, d3)
    permute(3)
    rest = bt[2, pl.ds(mine, HALF), :] - total.astype(F32)
    arrived(xp3, "xp3")
    for q in range(3):
        rest = rest - xp3[q].astype(F32)
    for h in (0, 1):
        xs[1, h] = scatter_done("rsf3", h, sf3, rf3).astype(BF16)
        swap("xf3", h, xs.at[1, h], xr3.at[h], 6)
    for h in (0, 1):
        arrived(xr3.at[h], f"xf3{h}")
        gather("agf3", h, rows_of(rest, h) - (xs[1, h].astype(F32) + xr3[h].astype(F32)), vf3)

    def keep(level, xo_ref):
        rcopy(xo_ref.at[pl.ds(mine, HALF)], xo_ref.at[pl.ds(mine, HALF)], f"xo{level}", sib).start()
        sends.append((f"xo{level}", xo_ref.at[pl.ds(0, HALF)]))

    def write(level, xo_ref):
        arrived(xo_ref.at[pl.ds(0, HALF)], f"xo{level}")
        count = ROWS[level]
        member = lf & ((1 << level) - 1)
        tmp[...] = xo_ref[...].T
        out[pl.ds(STARTS[level], count), :] = tmp[pl.ds(pl.multiple_of(member * count, count), count), :]

    def down(level, xo_ref, s_ref, r_ref, v_ref):
        for h in (0, 1):
            total = scatter_done(f"rsb{level}", h, s_ref, r_ref)
            gather(f"agb{level}", h, total, v_ref)
            xo_ref[part(h), :] = total
        keep(level, xo_ref)

    for h in (0, 1):
        y3 = dot_nt(gather_done("agf3", h, vf3), p3[...])
        scatter("rsb3", h, dot_nn(y3.astype(BF16), p3[...]), sb3, rb3)
    down(3, xo3, sb3, rb3, vb3)

    for h in (0, 1):
        z = y2[h] - dot_nt(gather_done("agb3", h, vb3), x23[...])
        scatter("rsb2", h, dot_nn(z.astype(BF16), p2[...]), sb2, rb2)
    v = both([whole(vb3, 0), whole(vb3, 1)])
    z1 = y1 - dot_nt(v, x13[...])
    t0 = dot_nt(v, x0[2])
    write(3, xo3)
    down(2, xo2, sb2, rb2, vb2)

    for h in (0, 1):
        z = rows_of(z1, h) - dot_nt(gather_done("agb2", h, vb2), x12[...])
        scatter("rsb1", h, dot_nn(z.astype(BF16), p1[...]), sb1, rb1)
    t0 = t0 + dot_nt(both([whole(vb2, 0), whole(vb2, 1)]), x0[1])
    write(2, xo2)
    down(1, xo1, sb1, rb1, vb1)

    def finish0(name, h, start, z):
        value = dot_nn(z.astype(BF16), d0[...])
        count = z.shape[0]
        place = pl.ds(pl.multiple_of(start + h * PART, PART), count)
        for b in range(BLKS):
            s0[b, place, :] = value[:, b * BLK : (b + 1) * BLK].astype(BF16)
        plane_push(f"{name}{h}", lambda k, p: s0.at[p, place], lambda k, p: r0.at[k, place])
        sends.append((f"{name}{h}", r0.at[:, pl.ds(0, count)]))

    for h in (0, 1):
        t = rows_of(t0, h) + dot_nt(gather_done("agb1", h, vb1), x0[0])
        ssend[h] = t[:, BLK:].astype(BF16)
        swap("sx", h, ssend.at[h], srecv.at[h], 1)
        finish0("rs0a", h, mine, y0r[part(h), :] - t[:, :BLK])
    for h in (0, 1):
        arrived(srecv.at[h], f"sx{h}")
    finish0("rs0b", 0, other, y0r[pl.ds(other, HALF), :] - both([srecv[0], srecv[1]]).astype(F32))
    write(1, xo1)
    last = {"rs0a0": PART, "rs0a1": PART, "rs0b0": HALF}
    for name, ref in sends:
        if name not in last:
            rcopy(ref, ref, name, sib).wait_send()
    for name in last:
        arrived(r0.at[:, pl.ds(0, last[name])], name)
    total = s0[bk].astype(F32)
    for k in range(BLKS - 1):
        total = total + r0[k].astype(F32)
    out[pl.ds(0, 128), :] = total.T
    for name, ref in sends:
        if name in last:
            rcopy(ref, ref, name, sib).wait_send()


def local(right_side, inverse_blocks, coupling, update_rows):
    def vm(*shape, t=BF16):
        return pltpu.VMEM(shape, t)

    block, part = (HALF, BLK), (PART, BLK)
    scratch = (
        [vm(128, CASES, t=F32), vm(34, UPD, t=jnp.int32)]
        + [vm(128, W)] * 7
        + [vm(128, UPD)] * 6
        + [vm(3, 256, W)]
        + [vm(128, W)] * 3
        + [vm(128, CASES, t=F32)] * 3
        + [vm(3, CASES, BLK, t=F32), vm(BLKS, CASES, BLK)]
        + [vm(CASES, BLK, t=F32), vm(*block), vm(*block)]
        + ([vm(2, BLKS, *part)] * 3 + [vm(2, BLKS - 1, *part)] * 3 + [vm(2, BLKS, *part)] * 3) * 2
        + [vm(2, 2, *part), vm(2, *part), vm(2, *part)]
        + [vm(*block), vm(3, *block), vm(BLKS, *block), vm(BLKS - 1, *block)]
        + [vm(2, *part), vm(2, *part)]
        + [vm(BLKS, CASES, BLK), vm(BLKS - 1, CASES, BLK)]
        + [vm(CASES, BLK, t=F32)] * 3
        + [vm(BLK, CASES, t=F32)]
        + [pltpu.SemaphoreType.DMA((len(NAMES),))] * 2
        + [pltpu.SemaphoreType.DMA((len(LOCALS),))]
    )
    result = pl.pallas_call(
        kernel,
        out_shape=jax.ShapeDtypeStruct((240, CASES), F32),
        in_specs=[pl.BlockSpec(memory_space=pltpu.HBM)] * 4,
        out_specs=pl.BlockSpec(memory_space=pltpu.VMEM),
        scratch_shapes=scratch,
        compiler_params=pltpu.CompilerParams(
            collective_id=0, has_side_effects=True, vmem_limit_bytes=56413184
        ),
        name="tree_solve",
    )(right_side[0, 0], inverse_blocks[0, 0], coupling[0, 0], update_rows)
    return result[None, None]


def solution(mesh):
    in_specs = (
        P("leaf", "blk", None, None),
        P("leaf", "blk", None, None),
        P("leaf", "blk", None, None),
        P(),
    )
    out_specs = P("leaf", "blk", None, None)
    return jax.shard_map(local, mesh=mesh, in_specs=in_specs, out_specs=out_specs, check_vma=False)
```
